256 devices in a mesh: group: 16 (over y, z_lo), expert: 16 (over x, z_hi, core).
Axes of the slice: x: 4, y: 4, z: 8 (z_hi: 2, z_lo: 4; z = z_hi * 4 + z_lo), core: 2. Of those that a mesh axis runs over, the one named last changes fastest.
Arguments:
- rows_in: bfloat16 [16384, 3584], P(('group', 'expert')), may hold values from -6 to 6
- expert_ids: int32 [16384, 2], P(('group', 'expert')), may hold values from 0 to 7, all different within a row; in each aligned block of 64 rows (0 to 63, 64 to 127, ...) at most 32 rows name the same one
- route_weight: float32 [16384, 2], P(('group', 'expert')), may hold values from 0.2 to 1
- gate_weight: bfloat16 [16, 3584, 512], P('expert'), may hold values from -0.09375 to 0.09375
- up_weight: bfloat16 [16, 3584, 512], P('expert'), may hold values from -0.09375 to 0.09375
- down_weight: bfloat16 [16, 512, 3584], P('expert'), may hold values from -0.1875 to 0.1875
- gate_b: bfloat16 [8, 3584, 64], P(None, 'group'), may hold values from -2 to 2
- gate_a: bfloat16 [16, 64, 512], P('expert', 'group'), may hold values from -0.15625 to 0.15625
- up_b: bfloat16 [8, 3584, 64], P(None, 'group'), may hold values from -2 to 2
- up_a: bfloat16 [16, 64, 512], P('expert', 'group'), may hold values from -0.15625 to 0.15625
- down_b: bfloat16 [16, 512, 64], P('expert', 'group'), may hold values from -2 to 2
- down_a: bfloat16 [8, 64, 3584], P(None, None, 'group'), may hold values from -0.25 to 0.25
Outputs:
- mixed: bfloat16 [16384, 3584], P(('group', 'expert'))
The draws below stay inside these ranges and needn't reach their ends.
Inputs may be any that keep to these rules, and one draw needn't show every extreme that they name: `expert_ids`: each row names 2 different experts. Within each aligned block of 64 rows (the rows of one device) no expert is named by more than 32 rows, a bound that some block reaches.
All inputs are finite; a program needn't handle non-finite values.
Results may differ from the reference program's by a relative error of at most 0.0076.
Values may be sent and summed in bfloat16 or wider, within the bound.
A program may use at most 128 MiB of HBM per device.

```python
import math
import jax
import jax.numpy as jnp
import numpy as np
from jax import lax

D = 3584
HID = 1024
RANK = 64
TOP = 2
ROWS_DEV = 64
HID_DEV = 512
EXPERTS = 8
CAP = 32
ROWS = 16384
N_EXPERT = 16


def block_scale(key, extent, pieces, smallest, top_value):
    def one(dim, blocks):
        heights = jax.random.uniform(jax.random.fold_in(jax.random.fold_in(key, 6), dim), (blocks,), jnp.float32, smallest / len(pieces), top_value / len(pieces))
        return jnp.repeat(jnp.exp(heights), extent[dim] // blocks).reshape((-1,) + (1,) * (len(extent) - dim - 1))

    level = one(*pieces[0])
    for cut in pieces[1:]:
        level = level * one(*cut)
    return level


def assign_block(key, own, number, rows, number_of, top, limit, slope):
    ranking = jax.random.permutation(key, number_of)
    packed, common = portions_of(number_of, rows * top, limit, slope, True), portions_of(number_of, rows * top, limit, slope, False)
    places = jnp.arange(number_of)

    def named(sizes, turn):
        used = int((sizes > 0).sum())
        fixed = max(1, used // 4)
        passed = fixed + (places - fixed + turn * (used - fixed)) % max(1, number_of - fixed)
        return jnp.zeros((number_of,), jnp.int32).at[ranking[jnp.where(places < fixed, places, passed)]].set(jnp.asarray(sizes, jnp.int32))

    sizes = jnp.where(number % 4 == 0, named(packed, number // 4), named(common, number - number // 4 - 1))
    mixed = jax.random.permutation(jax.random.fold_in(own, 3), number_of)
    giver, sink = mixed[0:number_of // 2 * 2:2], mixed[1:number_of // 2 * 2:2]
    margin = jnp.minimum(sizes[giver] - 1, limit - sizes[sink]) // 2
    margin = jnp.where((giver == ranking[0]) | (sink == ranking[0]) | (sizes[sink] == 0), 0, jnp.maximum(margin, 0))
    passed = jax.random.randint(jax.random.fold_in(own, 4), (number_of // 2,), 0, 1 << 20) % (margin + 1)
    sizes = sizes.at[giver].add(-passed).at[sink].add(passed)
    members = jnp.searchsorted(jnp.cumsum(sizes), jnp.arange(rows * top), side="right").astype(jnp.int32)
    listing = members.reshape(top, rows).T
    listing = listing[jax.random.permutation(jax.random.fold_in(own, 1), rows)]
    turn = jax.random.randint(jax.random.fold_in(own, 2), (rows, 1), 0, top)
    return jnp.take_along_axis(listing, (jnp.arange(top)[None, :] + turn) % top, axis=1)


def portions_of(number_of, total, most, slope, full):
    loads = [(1 << 20) // math.isqrt(rank ** slope) + 1 for rank in range(1, number_of + 1)]
    largest = most if full else min(most, max(-(-total // number_of), total * loads[0] // sum(loads)))
    least = 1 if total - largest >= number_of - 1 else 0
    holding, surplus = [largest] + [least] * (number_of - 1), total - largest - least * (number_of - 1)
    while surplus > 0:
        free = [i for i in range(1, number_of) if holding[i] < largest] or [i for i in range(1, number_of) if holding[i] < most]
        pool, left = sum([loads[i] for i in free]), surplus
        for i in free:
            more = min(most - holding[i], max(1, left * loads[i] // pool), surplus)
            holding[i] = holding[i] + more
            surplus = surplus - more
    return np.array(holding)


def gaussian(own_key, shape, scale, most, shards=(), kind=jnp.bfloat16):
    result = scale * jax.random.normal(own_key, shape, jnp.float32)
    if shards:
        result = result * block_scale(own_key, shape, shards, -0.22, 0.18)
    return jnp.clip(result, -most, most).astype(kind)


def setup_inputs(seed: int = 0) -> dict:
    seeds = jax.random.split(jax.random.key(seed), 13)
    rows_in = gaussian(seeds[0], (ROWS, D), 1.0, 6.0, ((0, 256),))
    expert_ids_keys = jax.random.split(jax.random.fold_in(seeds[1], 1), ROWS // ROWS_DEV)
    expert_ids_turns = jax.random.permutation(jax.random.fold_in(seeds[1], 3), ROWS // ROWS_DEV)
    expert_ids = jax.vmap(lambda own, number: assign_block(jax.random.fold_in(seeds[1], 2), own, number, ROWS_DEV, EXPERTS, TOP, CAP, 2))(expert_ids_keys, expert_ids_turns).reshape((ROWS, TOP))
    route_weight = jnp.clip(jnp.exp(math.log(1.0) - 1.609438 * jax.random.uniform(seeds[2], (ROWS, TOP), jnp.float32) ** block_scale(seeds[2], (ROWS, TOP), ((0, 256),), -0.2, 0.2)), 0.2, 1.0)
    gate_weight = gaussian(seeds[3], (N_EXPERT, D, HID_DEV), D ** -0.5, 0.09375, ((0, 16),))
    up_weight = gaussian(seeds[4], (N_EXPERT, D, HID_DEV), D ** -0.5, 0.09375, ((0, 16),))
    down_weight = gaussian(seeds[5], (N_EXPERT, HID_DEV, D), HID ** -0.5, 0.1875, ((0, 16),))
    gate_b = gaussian(seeds[6], (EXPERTS, D, RANK), (RANK ** -0.5), 2.0, ((1, 16),))
    gate_a = gaussian(seeds[7], (N_EXPERT, RANK, HID_DEV), (0.6 * D ** -0.5), 0.15625, ((0, 16), (1, 16)))
    up_b = gaussian(seeds[8], (EXPERTS, D, RANK), (RANK ** -0.5), 2.0, ((1, 16),))
    up_a = gaussian(seeds[9], (N_EXPERT, RANK, HID_DEV), (0.6 * D ** -0.5), 0.15625, ((0, 16), (1, 16)))
    down_b = gaussian(seeds[10], (N_EXPERT, HID_DEV, RANK), (RANK ** -0.5), 2.0, ((0, 16), (1, 16)))
    down_a = gaussian(seeds[11], (EXPERTS, RANK, D), (0.6 * HID ** -0.5), 0.25, ((2, 16),))
    return dict(rows_in=rows_in, expert_ids=expert_ids, route_weight=route_weight, gate_weight=gate_weight, up_weight=up_weight, down_weight=down_weight, gate_b=gate_b, gate_a=gate_a, up_b=up_b, up_a=up_a, down_b=down_b, down_a=down_a)


def reference(rows_in, expert_ids, route_weight, gate_weight, up_weight, down_weight, gate_b, gate_a, up_b, up_a, down_b, down_a):
    blocks = ROWS // ROWS_DEV
    local = jnp.arange(ROWS_DEV, dtype=jnp.int32)
    slots = jnp.arange(CAP, dtype=jnp.int32)
    starts = jnp.arange(blocks, dtype=jnp.int32) * ROWS_DEV

    def one_expert(total, expert):
        named = (expert_ids == expert)
        hits = jnp.sum(named.astype(jnp.int32), axis=1).reshape(blocks, ROWS_DEV)
        place = jnp.cumsum(hits, axis=1) - hits
        table_hit = ((hits[:, :, None] == 1) & (place[:, :, None] == slots[None, None, :])).astype(jnp.int32)
        table = jnp.sum(table_hit * local[None, :, None], axis=1)
        valid = jnp.sum(table_hit, axis=1)
        index = (table + starts[:, None]).reshape(-1).astype(jnp.int32)
        chosen = rows_in[index]
        row_weight = jnp.sum(route_weight * named.astype(jnp.float32), axis=1)[index] * valid.reshape(-1).astype(jnp.float32)
        partial_value = jnp.zeros((blocks * CAP, D), jnp.float32)
        for half in range(2):
            slice_id = 2 * expert + half
            merged_gate = (gate_weight[slice_id] + jnp.dot(gate_b[expert], gate_a[slice_id], preferred_element_type=jnp.float32)).astype(jnp.bfloat16)
            merged_up = (up_weight[slice_id] + jnp.dot(up_b[expert], up_a[slice_id], preferred_element_type=jnp.float32)).astype(jnp.bfloat16)
            merged_down = (down_weight[slice_id] + jnp.dot(down_b[slice_id], down_a[expert], preferred_element_type=jnp.float32)).astype(jnp.bfloat16)
            gate_part = jnp.dot(chosen, merged_gate, preferred_element_type=jnp.float32)
            up_part = jnp.dot(chosen, merged_up, preferred_element_type=jnp.float32)
            hidden_part = (jax.nn.silu(gate_part) * up_part).astype(jnp.bfloat16)
            partial_value = partial_value + jnp.dot(hidden_part, merged_down, preferred_element_type=jnp.float32)
        expert_out = lax.optimization_barrier(partial_value.astype(jnp.bfloat16)).astype(jnp.float32)
        total = total.at[index].add(row_weight[:, None] * expert_out)
        return total, None

    total, unused = lax.scan(one_expert, jnp.zeros((ROWS, D), jnp.float32), jnp.arange(EXPERTS, dtype=jnp.int32))
    return total.astype(jnp.bfloat16)
```

```python
import jax
import jax.numpy as jnp
from jax import lax
from jax.experimental import pallas as pl
from jax.experimental.pallas import tpu as pltpu
from jax.sharding import PartitionSpec as P

MESH = pl.DeviceIdType.MESH
BF = jnp.bfloat16
F32 = jnp.float32

D = 3584
HID = 512
ROWS = 64
CAP = 32
RANK = 64
KC = 512
NK = D // KC
HALF = D // 2
JC = 256
NJ = HALF // JC
SHARD = 224
PART = SHARD // 2


def iota(shape, dim):
    return lax.broadcasted_iota(jnp.int32, shape, dim)


def onehot(mask):
    return jnp.where(mask, 1.0, 0.0).astype(BF)


def dot(a, b):
    return jnp.dot(a, b, preferred_element_type=F32)


def dot_nt(a, b):
    return lax.dot_general(a, b, (((1,), (1,)), ((), ())), preferred_element_type=F32)


def split(v):
    high = v.astype(BF)
    return high, (v - high.astype(F32)).astype(BF)


def kernel(
    rows, ids, wts, gate_w, up_w, down_w, gate_b, gate_a, up_b, up_a, down_b, down_a,
    out,
    rw, meta, tab, wtab, sel, got, w, dw, acc, low, hid, back, back_got,
    pack_g, pack_u, pack_d, fac, gub, daf, dbf, a2,
    zs, zr, own, fin, fin_got,
    s_load, s_w, s_dw, s_meta, s_zrow, r_zrow, r_meta,
    s_x, r_x, s_fwd, r_fwd, s_dwx, r_dwx, s_fac, r_facz, r_facy, r_facd,
    s_hid, r_hid, s_ret, r_ret, s_zret, r_zret, s_fin, r_fin,
):
    g = lax.axis_index("group")
    e = lax.axis_index("expert")
    y, zl = g // 4, g % 4
    x, zh, c = e // 4, (e // 2) % 2, e % 2
    pair = e // 2

    def dev(y_, zl_, x_, zh_, c_):
        return (y_ * 4 + zl_, (x_ * 2 + zh_) * 2 + c_)

    sibling = dev(y, zl, x, zh, 1 - c)
    mirror = dev(y, 3 - zl, x, 1 - zh, c)
    x_up = [dev(y, zl, (x + d) % 4, zh, c) for d in (1, 2, 3)]
    x_down = [dev(y, zl, (x + 4 - d) % 4, zh, c) for d in (1, 2, 3)]
    z_peers = [dev(y, (zl + d) % 4, x, zh, c) for d in (1, 2, 3)]
    y_peers = [dev((y + d) % 4, zl, x, zh, c) for d in (1, 2, 3)]
    far = jnp.where((zl == 1) | (zl == 2), 1, 0)
    first, second = far, 1 - far

    def remote(src, dst, ssem, rsem, target):
        return pltpu.make_async_remote_copy(
            src_ref=src, dst_ref=dst, send_sem=ssem, recv_sem=rsem,
            device_id=target, device_id_type=MESH)

    def wait_bytes(ref, sem):
        pltpu.make_async_copy(ref, ref, sem).wait()

    loads = [
        pltpu.make_async_copy(gate_b.at[pair], pack_g, s_load.at[0]),
        pltpu.make_async_copy(up_b.at[pair], pack_u, s_load.at[1]),
        pltpu.make_async_copy(down_a.at[pair], pack_d, s_load.at[2]),
    ]
    for copy in loads:
        copy.start()

    def row_load(k):
        return pltpu.make_async_copy(
            rows.at[:, pl.ds(pl.multiple_of(k * KC, KC), KC)], rw.at[0, k], s_load.at[3 + k])

    def w_load(k, part):
        src = (gate_w, up_w)[part]
        return pltpu.make_async_copy(
            src.at[0, pl.ds(pl.multiple_of(k * KC, KC), KC), :],
            w.at[k, :, pl.ds(part * HID, HID)], s_w.at[k, part])

    def dw_cols(core, j):
        return down_w.at[0, :, pl.ds(pl.multiple_of(core * HALF + j * JC, JC), JC)]

    def dw_load(j):
        return pltpu.make_async_copy(dw_cols(c, j), dw.at[c, j], s_dw.at[j])

    def dw_send(j):
        return remote(dw_cols(1 - c, j), dw.at[c, j], s_dwx.at[j], r_dwx.at[j], sibling)

    @pl.loop(0, NK)
    def _(k):
        row_load(k).start()

    @pl.loop(0, NK)
    def _(k):
        w_load(k, 0).start()
        w_load(k, 1).start()

    barrier = pltpu.get_barrier_semaphore()
    peers = [sibling, mirror] + x_up + z_peers + y_peers
    for peer in peers:
        pl.semaphore_signal(barrier, inc=1, device_id=peer, device_id_type=MESH)

    lane = iota((ROWS, 128), 1)
    idf = ids[...].astype(F32)
    wt = wts[...]
    meta[0, c] = jnp.where(
        lane == 0, idf[:, 0:1],
        jnp.where(lane == 1, idf[:, 1:2], jnp.where(lane == 2, wt[:, 0:1], wt[:, 1:2])))

    pl.semaphore_wait(barrier, len(peers))

    meta_mirror = remote(meta.at[0, c], meta.at[1, c], s_meta.at[0], r_meta.at[0], mirror)
    meta_sibling = remote(meta.at[0, c], meta.at[0, c], s_meta.at[1], r_meta.at[1], sibling)
    meta_second = remote(meta.at[1, c], meta.at[1, c], s_meta.at[2], r_meta.at[2], sibling)
    meta_mirror.start()
    meta_sibling.start()

    def zrow(k):
        return remote(
            rows.at[:, pl.ds(pl.multiple_of(k * KC, KC), KC)], rw.at[1, k],
            s_zrow.at[k], r_zrow.at[k], mirror)

    @pl.when(far == 0)
    def _():
        @pl.loop(0, NK)
        def _(k):
            zrow(k).start()

    for copy in loads:
        copy.wait()
    half = pl.ds(pl.multiple_of(c * PART, 16), PART)
    left64 = onehot(iota((64, 128), 0) == iota((64, 128), 1))
    right64 = onehot(iota((64, 128), 0) + 64 == iota((64, 128), 1))
    packed = dot(pack_g[half, :], left64) + dot(pack_u[half, :], right64)
    mine = fac.at[y, zl, c]
    mine[:, 0:128] = packed.astype(BF)
    pick = onehot(iota((PART, SHARD), 1) == iota((PART, SHARD), 0) + c * PART)
    turned = dot_nt(pick, pack_d[...]).astype(BF)
    placed = dot(onehot(iota((PART, 32), 0) == iota((PART, 32), 1)), down_b[0]).astype(BF)
    row = iota((PART, 4), 0) - 32
    fits = (row >= 0) & (row < 64)
    which = (row + 32) % 8
    col = iota((PART, 4), 1)
    spread = (dot(onehot(fits & (which == col)), gate_a[0])
              + dot(onehot(fits & (which == col + 4)), up_a[0]))
    block = (iota((PART, HID), 0) - 32) // 8
    spread = jnp.where(block == iota((PART, HID), 1) // 64, spread, 0.0).astype(BF)
    fold = onehot(iota((HID, 128), 0) % 64 + 64 == iota((HID, 128), 1))
    packed = dot(turned, left64) + dot(placed, right64) + dot(spread, fold)
    mine[:, 128:256] = packed.astype(BF)

    for d in range(3):
        remote(fac.at[y, zl, c], fac.at[y, zl, c], s_fac.at[0], r_facz, z_peers[d]).start()

    @pl.when(far == 1)
    def _():
        @pl.loop(0, NK)
        def _(k):
            zrow(k).start()

    @pl.loop(0, NJ)
    def _(j):
        dw_load(j).start()
        dw_send(j).start()

    def tables(m):
        lane = iota((ROWS, 128), 1)
        expert = (((x + lane // 32) % 4) * 2 + zh).astype(F32)
        hit0, hit1 = m[:, 0:1] == expert, m[:, 1:2] == expert
        hit = jnp.where(hit0, 1.0, 0.0) + jnp.where(hit1, 1.0, 0.0)
        before = onehot(iota((ROWS, ROWS), 1) < iota((ROWS, ROWS), 0))
        place = dot(before, hit.astype(BF))
        table = jnp.where(place == (lane % 32).astype(F32), hit, 0.0)
        weight = jnp.where(hit0, m[:, 2:3], 0.0) + jnp.where(hit1, m[:, 3:4], 0.0)
        return table, table * weight

    def make_select(om):
        table, weight = tables(meta[om, c])
        tab[om] = table.T.astype(BF)
        high, rest = split(weight)
        wtab[om, c, 0:ROWS, :] = high
        wtab[om, c, ROWS:2 * ROWS, :] = rest

    def make_weights(om, cs):
        _, weight = tables(meta[om, cs])
        high, rest = split(weight)
        wtab[om, cs, 0:ROWS, :] = high
        wtab[om, cs, ROWS:2 * ROWS, :] = rest

    def dispatch(om, k):
        @pl.when(om == 0)
        def _():
            row_load(k).wait()

        @pl.when(om == 1)
        def _():
            zrow(k).wait_recv()

        value = dot(tab[om], rw[om, k]).astype(BF)
        got[om, k, 0, c] = value[0:CAP]
        sel[om, k] = value[CAP:].reshape(3, CAP, KC)
        for d in range(3):
            remote(sel.at[om, k, d], got.at[om, k, d + 1, c], s_x, r_x.at[om, k], x_up[d]).start()

    def forward(om, k):
        return remote(got.at[om, k, :, c], got.at[om, k, :, c],
                      s_fwd.at[om, k], r_fwd.at[om, k], sibling)

    def arrive(om, k):
        wait_bytes(sel.at[om, k], r_x.at[om, k])
        forward(om, k).start()

    def gate_up(om, k):
        forward(om, k).wait_recv()
        value = got[om, k].reshape(8 * CAP, KC)
        for n in range(4):
            cols = pl.ds(n * 256, 256)
            part = dot(value, w[k, :, cols])

            @pl.when(k == 0)
            def _():
                acc[om, :, cols] = part

            @pl.when(k > 0)
            def _():
                acc[om, :, cols] += part

    make_select(0)

    @pl.when(far == 1)
    def _():
        meta_mirror.wait_recv()
        meta_second.start()
        make_select(1)

    @pl.loop(0, 3)
    def _(k):
        dispatch(first, k)

    wait_bytes(fac.at[0, pl.ds(0, 3), 0], r_facz)
    for d in range(3):
        remote(fac.at[y, :, c], fac.at[y, :, c], s_fac.at[1], r_facy, y_peers[d]).start()

    @pl.loop(3, NK)
    def _(k):
        dispatch(first, k)

    @pl.when(far == 0)
    def _():
        meta_mirror.wait_recv()
        meta_second.start()
        make_select(1)

    @pl.loop(0, NK + 1)
    def _(k):
        @pl.when(k < NK)
        def _():
            dispatch(second, k)
            arrive(first, k)
            w_load(k, 0).wait()
            w_load(k, 1).wait()

        @pl.when(k > 0)
        def _():
            gate_up(first, k - 1)

    wait_bytes(fac.at[pl.ds(0, 3), :, 0], r_facy)
    fac_forward = remote(fac.at[:, :, c], fac.at[:, :, c], s_fac.at[2], r_facd, sibling)
    fac_forward.start()
    meta_sibling.wait_recv()
    meta_second.wait_recv()
    make_weights(0, 1 - c)
    make_weights(1, 1 - c)
    fac_forward.wait_recv()

    left = iota((896, 128), 1) < 64
    for yy in range(4):
        gub[pl.ds(yy * 896, 896), :] = fac[yy, :, :, :, 0:128].reshape(896, 128)
        part = fac[yy, :, :, :, 128:256].reshape(896, 128).astype(F32)
        part = jnp.where(left, part, 0.0)
        daf[pl.ds(yy * 896, 896), :] = (part + pltpu.roll(part, 64, 1)).astype(BF)
        for core in range(2):
            part = fac[yy, :, core, 0:32, 128:256].reshape(128, 128)
            dbf[core, pl.ds(yy * 128, 128), :] = jnp.where(
                iota((128, 128), 1) < 64, jnp.zeros_like(part), part)
    small = fac[:, :, c, 32:96, 128:256].reshape(1024, 128)
    unfold = onehot((iota((128, HID), 1) % 64 + 64) == iota((128, HID), 0))
    wide = dot(small, unfold)
    block = (iota((1024, HID), 0) % 64) // 8
    wide = jnp.where(block == iota((1024, HID), 1) // 64, wide, 0.0).astype(BF)
    r = iota((128, 1024), 0)
    s = iota((128, 1024), 1)
    take = onehot((s // 64 == (r % 64) // 4) & (s % 8 == r % 4 + 4 * (r // 64)))
    right = dot(take, wide).astype(BF)
    upper = iota((128, HID), 0) < 64
    for n in range(2):
        rs = pl.ds(n * 128, 128)
        a2[rs, 0:HID] = jnp.where(upper, right, jnp.zeros_like(right))
        a2[rs, HID:2 * HID] = jnp.where(upper, jnp.zeros_like(right), right)

    def hidden(om):
        low[...] = jnp.zeros_like(low)

        @pl.loop(0, NK)
        def _(k):
            low[...] += dot(got[om, k].reshape(8 * CAP, KC),
                            gub[pl.ds(pl.multiple_of(k * KC, KC), KC), :])

        high, rest = split(low[...])
        both = jnp.concatenate([high, rest], axis=1)
        for n in range(2):
            cols, ups = pl.ds(n * 256, 256), pl.ds(HID + n * 256, 256)
            gate = acc[om, :, cols] + dot(both, a2[:, cols])
            up = acc[om, :, ups] + dot(both, a2[:, ups])
            hid[om, c, :, cols] = (gate / (1.0 + jnp.exp(-gate)) * up).astype(BF)
        hid_send(om).start()

    def hid_send(om):
        return remote(hid.at[om, c], hid.at[om, c], s_hid.at[om], r_hid.at[om], sibling)

    def low_down(om):
        hid_send(om).wait_recv()
        value = dot(hid[om, 0], dbf[0]) + dot(hid[om, 1], dbf[1])
        high, rest = split(value)
        low2 = high.astype(F32) + pltpu.roll(rest.astype(F32), 64, 1)
        return low2.astype(BF)

    def down(om, j, low2):
        da = daf[pl.ds(pl.multiple_of(c * HALF + j * JC, JC), JC), :]
        value = dot(hid[om, 0], dw[0, j]) + dot(hid[om, 1], dw[1, j]) + dot_nt(low2, da)
        value = value.astype(BF).reshape(4, 2, CAP, JC)
        back_got[om, j, 0] = value[0]
        back[om, j] = value[1:]
        for d in range(3):
            remote(back.at[om, j, d], back_got.at[om, j, d + 1],
                   s_ret, r_ret.at[om, j], x_down[d]).start()

    def zret(j):
        return remote(zs.at[j], zr.at[j], s_zret.at[j], r_zret.at[j], mirror)

    def combine(om, j):
        wait_bytes(back.at[om, j], r_ret.at[om, j])
        for cs in range(2):
            value = dot(wtab[om, cs], back_got[om, j, :, cs].reshape(4 * CAP, JC))
            value = value[0:ROWS] + value[ROWS:]

            @pl.when(om == 0)
            def _():
                own[j, cs] = value

            @pl.when(om == 1)
            def _():
                zs[j, cs] = value.astype(BF)

        @pl.when(om == 1)
        def _():
            zret(j).start()

    def fin_send(j):
        return remote(fin.at[j], fin_got.at[j], s_fin.at[j], r_fin.at[j], sibling)

    def finish(j):
        zret(j).wait_recv()
        fin[j] = (own[j, 1 - c] + zr[j, 1 - c].astype(F32)).astype(BF)
        fin_send(j).start()
        cols = pl.ds(pl.multiple_of(c * HALF + j * JC, JC), JC)
        out[:, cols] = (own[j, c] + zr[j, c].astype(F32)).astype(BF)

    hidden(first)

    @pl.loop(0, NJ)
    def _(j):
        dw_load(j).wait()
        dw_send(j).wait_recv()

    low_first = low_down(first)

    @pl.loop(0, NK + 1)
    def _(k):
        @pl.when(k < NK)
        def _():
            arrive(second, k)
            down(first, k, low_first)

        @pl.when(k > 0)
        def _():
            gate_up(second, k - 1)

    hidden(second)

    @pl.loop(0, 3)
    def _(j):
        combine(first, j)

    low_second = low_down(second)

    @pl.loop(0, NJ)
    def _(j):
        down(second, j, low_second)

        @pl.when(j + 3 < NJ)
        def _():
            combine(first, j + 3)

    @pl.loop(0, NJ)
    def _(j):
        combine(second, j)

    @pl.loop(0, NJ)
    def _(j):
        finish(j)

    @pl.loop(0, NJ)
    def _(j):
        fin_send(j).wait_recv()
        cols = pl.ds(pl.multiple_of((1 - c) * HALF + j * JC, JC), JC)
        out[:, cols] = fin_got[j]

    meta_mirror.wait_send()
    meta_sibling.wait_send()
    meta_second.wait_send()
    wait_bytes(sel, s_x)
    wait_bytes(back, s_ret)
    wait_bytes(fac.at[0, pl.ds(0, 3), 0], s_fac.at[0])
    wait_bytes(fac.at[pl.ds(0, 3), :, 0], s_fac.at[1])
    fac_forward.wait_send()
    for om in range(2):
        hid_send(om).wait_send()

        @pl.loop(0, NK)
        def _(k):
            forward(om, k).wait_send()

    @pl.loop(0, NJ)
    def _(j):
        zrow(j).wait_send()
        dw_send(j).wait_send()
        zret(j).wait_send()
        fin_send(j).wait_send()


def on_device(*args):
    vmem = pl.BlockSpec(memory_space=pltpu.VMEM)
    hbm = pl.BlockSpec(memory_space=pl.ANY)
    dma = pltpu.SemaphoreType.DMA
    scratch = [
        pltpu.VMEM((2, NK, ROWS, KC), BF),
        pltpu.VMEM((2, 2, ROWS, 128), F32),
        pltpu.VMEM((2, 128, ROWS), BF),
        pltpu.VMEM((2, 2, 2 * ROWS, 128), BF),
        pltpu.VMEM((2, NK, 3, CAP, KC), BF),
        pltpu.VMEM((2, NK, 4, 2, CAP, KC), BF),
        pltpu.VMEM((NK, KC, 2 * HID), BF),
        pltpu.VMEM((2, NJ, HID, JC), BF),
        pltpu.VMEM((2, 8 * CAP, 2 * HID), F32),
        pltpu.VMEM((8 * CAP, 128), F32),
        pltpu.VMEM((2, 2, 8 * CAP, HID), BF),
        pltpu.VMEM((2, NJ, 3, 2, CAP, JC), BF),
        pltpu.VMEM((2, NJ, 4, 2, CAP, JC), BF),
        pltpu.VMEM((SHARD, RANK), BF),
        pltpu.VMEM((SHARD, RANK), BF),
        pltpu.VMEM((RANK, SHARD), BF),
        pltpu.VMEM((4, 4, 2, PART, 256), BF),
        pltpu.VMEM((D, 128), BF),
        pltpu.VMEM((D, 128), BF),
        pltpu.VMEM((2, HID, 128), BF),
        pltpu.VMEM((256, 2 * HID), BF),
        pltpu.VMEM((NJ, 2, ROWS, JC), BF),
        pltpu.VMEM((NJ, 2, ROWS, JC), BF),
        pltpu.VMEM((NJ, 2, ROWS, JC), F32),
        pltpu.VMEM((NJ, ROWS, JC), BF),
        pltpu.VMEM((NJ, ROWS, JC), BF),
        dma((3 + NK,)),
        dma((NK, 2)),
        dma((NJ,)),
        dma((3,)),
        dma((NK,)),
        dma((NK,)),
        dma((3,)),
        dma,
        dma((2, NK)),
        dma((2, NK)),
        dma((2, NK)),
        dma((NJ,)),
        dma((NJ,)),
        dma((3,)),
        dma,
        dma,
        dma,
        dma((2,)),
        dma((2,)),
        dma,
        dma((2, NJ)),
        dma((NJ,)),
        dma((NJ,)),
        dma((NJ,)),
        dma((NJ,)),
    ]
    return pl.pallas_call(
        kernel,
        out_shape=jax.ShapeDtypeStruct((ROWS, D), BF),
        in_specs=[hbm, vmem, vmem, hbm, hbm, hbm, hbm, vmem, hbm, vmem, vmem, hbm],
        out_specs=vmem,
        scratch_shapes=scratch,
        compiler_params=pltpu.CompilerParams(
            collective_id=0, has_side_effects=True, vmem_limit_bytes=48 << 20),
        cost_estimate=pl.CostEstimate(
            flops=8 << 30, bytes_accessed=13 << 20, transcendentals=1 << 18),
        name="expert_layer",
    )(*args)


def solution(mesh):
    return jax.shard_map(
        on_device,
        mesh=mesh,
        in_specs=(
            P(("group", "expert"), None),
            P(("group", "expert"), None),
            P(("group", "expert"), None),
            P("expert", None, None),
            P("expert", None, None),
            P("expert", None, None),
            P(None, "group", None),
            P("expert", "group", None),
            P(None, "group", None),
            P("expert", "group", None),
            P("expert", "group", None),
            P(None, None, "group"),
        ),
        out_specs=P(("group", "expert"), None),
        check_vma=False,
    )
```

```python
import jax
import jax.numpy as jnp
from jax import lax
from jax.experimental import pallas as pl
from jax.experimental.pallas import tpu as pltpu
from jax.sharding import PartitionSpec as P

MESH = pl.DeviceIdType.MESH
BF = jnp.bfloat16
F32 = jnp.float32

D = 3584
HID = 512
ROWS = 64
CAP = 32
RANK = 64
KC = 512
NK = D // KC
HALF = D // 2
JC = 256
NJ = HALF // JC
SHARD = 224
PART = SHARD // 2


def iota(shape, dim):
    return lax.broadcasted_iota(jnp.int32, shape, dim)


def onehot(mask):
    return jnp.where(mask, 1.0, 0.0).astype(BF)


def dot(a, b):
    return jnp.dot(a, b, preferred_element_type=F32)


def dot_nt(a, b):
    return lax.dot_general(a, b, (((1,), (1,)), ((), ())), preferred_element_type=F32)


def split(v):
    high = v.astype(BF)
    return high, (v - high.astype(F32)).astype(BF)


def kernel(
    rows, ids, wts, gate_w, up_w, down_w, gate_b, gate_a, up_b, up_a, down_b, down_a,
    out,
    rw, meta, tab, wtab, sel, got, w, dw, acc, low, hid, back, back_got,
    ids_v, wts_v, ga_v, ua_v, db_v, pack_g, pack_u, pack_d, fac_a, fac_b, gub, daf, dbf, a2,
    zs, zr, own, fin, fin_got,
    s_load, s_w, s_dw, s_meta, s_zrow, r_zrow, r_meta,
    s_x, r_x, s_fwd, r_fwd, s_dwx, r_dwx, s_fac, r_facz, r_facy, r_facd,
    s_hid, r_hid, s_ret, r_ret, s_zret, r_zret, s_fin, r_fin,
):
    g = lax.axis_index("group")
    e = lax.axis_index("expert")
    y, zl = g // 4, g % 4
    x, zh, c = e // 4, (e // 2) % 2, e % 2
    pair = e // 2

    def dev(y_, zl_, x_, zh_, c_):
        return (y_ * 4 + zl_, (x_ * 2 + zh_) * 2 + c_)

    sibling = dev(y, zl, x, zh, 1 - c)
    mirror = dev(y, 3 - zl, x, 1 - zh, c)
    x_up = [dev(y, zl, (x + d) % 4, zh, c) for d in (1, 2, 3)]
    x_down = [dev(y, zl, (x + 4 - d) % 4, zh, c) for d in (1, 2, 3)]
    z_peers = [dev(y, (zl + d) % 4, x, zh, c) for d in (1, 2, 3)]
    y_peers = [dev((y + d) % 4, zl, x, zh, c) for d in (1, 2, 3)]
    far = jnp.where((zl == 1) | (zl == 2), 1, 0)

    def remote(src, dst, ssem, rsem, target):
        return pltpu.make_async_remote_copy(
            src_ref=src, dst_ref=dst, send_sem=ssem, recv_sem=rsem,
            device_id=target, device_id_type=MESH)

    def wait_bytes(ref, sem):
        pltpu.make_async_copy(ref, ref, sem).wait()

    loads = [
        pltpu.make_async_copy(src, dst, s_load.at[NK + n]) for n, (src, dst) in enumerate((
            (ids, ids_v), (wts, wts_v), (gate_b.at[pair], pack_g), (up_b.at[pair], pack_u),
            (down_a.at[pair], pack_d), (gate_a, ga_v), (up_a, ua_v), (down_b, db_v)))
    ]
    for copy in loads:
        copy.start()

    def row_load(k):
        return pltpu.make_async_copy(
            rows.at[:, pl.ds(pl.multiple_of(k * KC, KC), KC)], rw.at[0, k], s_load.at[k])

    def w_load(k, part):
        src = (gate_w, up_w)[part]
        return pltpu.make_async_copy(
            src.at[0, pl.ds(pl.multiple_of(k * KC, KC), KC), :],
            w.at[k, :, pl.ds(part * HID, HID)], s_w.at[k, part])

    def dw_cols(core, j):
        return down_w.at[0, :, pl.ds(pl.multiple_of(core * HALF + j * JC, JC), JC)]

    def dw_load(j):
        return pltpu.make_async_copy(dw_cols(c, j), dw.at[c, j], s_dw.at[j])

    def dw_send(j):
        return remote(dw_cols(1 - c, j), dw.at[c, j], s_dwx.at[j], r_dwx.at[j], sibling)

    @pl.loop(0, NK)
    def _(k):
        row_load(k).start()

    @pl.loop(0, NK)
    def _(k):
        w_load(k, 0).start()
        w_load(k, 1).start()

    barrier = pltpu.get_barrier_semaphore()
    peers = [sibling, mirror] + x_up + z_peers + y_peers
    for peer in peers:
        pl.semaphore_signal(barrier, inc=1, device_id=peer, device_id_type=MESH)

    loads[0].wait()
    loads[1].wait()
    line = iota((128, ROWS), 0)
    idf = ids_v[...].astype(F32)
    named = jnp.where(
        line == 0, idf[0:1, :],
        jnp.where(line == 1, idf[1:2, :], jnp.where(line == 2, wts_v[0:1, :], wts_v[1:2, :])))
    meta[0, c] = named.T

    pl.semaphore_wait(barrier, len(peers))

    meta_mirror = remote(meta.at[0, c], meta.at[1, c], s_meta.at[0], r_meta.at[0], mirror)
    meta_sibling = remote(meta.at[0, c], meta.at[0, c], s_meta.at[1], r_meta.at[1], sibling)
    meta_second = remote(meta.at[1, c], meta.at[1, c], s_meta.at[2], r_meta.at[2], sibling)
    meta_mirror.start()
    meta_sibling.start()

    def zrow(k):
        return remote(
            rows.at[:, pl.ds(pl.multiple_of(k * KC, KC), KC)], rw.at[1, k],
            s_zrow.at[k], r_zrow.at[k], mirror)

    def tables(m):
        lane = iota((ROWS, 128), 1)
        expert = (((x + lane // 32) % 4) * 2 + zh).astype(F32)
        hit0, hit1 = m[:, 0:1] == expert, m[:, 1:2] == expert
        hit = jnp.where(hit0, 1.0, 0.0) + jnp.where(hit1, 1.0, 0.0)
        before = onehot(iota((ROWS, ROWS), 1) < iota((ROWS, ROWS), 0))
        place = dot(before, hit.astype(BF))
        table = jnp.where(place == (lane % 32).astype(F32), hit, 0.0)
        weight = jnp.where(hit0, m[:, 2:3], 0.0) + jnp.where(hit1, m[:, 3:4], 0.0)
        return table, table * weight

    def make_select(om):
        table, weight = tables(meta[om, c])
        tab[om] = table.T.astype(BF)
        high, rest = split(weight)
        wtab[om, c, 0:ROWS, :] = high
        wtab[om, c, ROWS:2 * ROWS, :] = rest

    def make_weights(om, cs):
        _, weight = tables(meta[om, cs])
        high, rest = split(weight)
        wtab[om, cs, 0:ROWS, :] = high
        wtab[om, cs, ROWS:2 * ROWS, :] = rest

    def dispatch(om, k):
        @pl.when(om == 0)
        def _():
            row_load(k).wait()

        @pl.when(om == 1)
        def _():
            zrow(k).wait_recv()

        value = dot(tab[om], rw[om, k]).astype(BF)
        got[om, k, 0, c] = value[0:CAP]
        sel[om, k] = value[CAP:].reshape(3, CAP, KC)
        for d in range(3):
            remote(sel.at[om, k, d], got.at[om, k, d + 1, c], s_x, r_x.at[om, k], x_up[d]).start()

    def forward(om, k):
        return remote(got.at[om, k, :, c], got.at[om, k, :, c],
                      s_fwd.at[om, k], r_fwd.at[om, k], sibling)

    def arrive(om, k):
        wait_bytes(sel.at[om, k], r_x.at[om, k])
        forward(om, k).start()

    def gate_up(om, k):
        forward(om, k).wait_recv()
        value = got[om, k].reshape(8 * CAP, KC)
        for n in range(4):
            cols = pl.ds(n * 256, 256)
            acc[om, :, cols] += dot(value, w[k, :, cols])

    def low_part(om, k):
        return dot(got[om, k].reshape(8 * CAP, KC),
                   gub[pl.ds(pl.multiple_of(k * KC, KC), KC), :])

    @pl.when(far == 0)
    def _():
        @pl.loop(0, NK)
        def _(k):
            zrow(k).start()

    for copy in loads[2:]:
        copy.wait()
    left64 = onehot(iota((64, 128), 0) == iota((64, 128), 1))
    right64 = onehot(iota((64, 128), 0) + 64 == iota((64, 128), 1))
    pick = onehot(iota((PART, SHARD), 1) == iota((PART, SHARD), 0) + c * PART)
    fac_a[y, zl, c, 0:PART, :] = (
        dot(dot_nt(pick, pack_g[...]).astype(BF), left64)
        + dot(dot_nt(pick, pack_u[...]).astype(BF), right64)).astype(BF)
    rights = jnp.concatenate([ga_v[0].astype(F32), ua_v[0].astype(F32)], axis=0)
    fac_a[y, zl, c, PART:PART + 32, :] = jnp.concatenate(
        [rights[:, 128 * q:128 * q + 128] for q in range(4)], axis=0).astype(BF)

    def fac_z(part):
        fac = (fac_a, fac_b)[part]
        for d in range(3):
            remote(fac.at[y, zl, c], fac.at[y, zl, c],
                   s_fac.at[part, 0], r_facz.at[part], z_peers[d]).start()

    fac_z(0)

    @pl.when(far == 1)
    def _():
        @pl.loop(0, NK)
        def _(k):
            zrow(k).start()

    make_select(0)

    @pl.loop(0, NK)
    def _(k):
        dispatch(0, k)

    turned = dot_nt(pick, pack_d[...]).astype(BF)
    placed = dot(onehot(iota((PART, 32), 0) == iota((PART, 32), 1)), db_v[0]).astype(BF)
    fac_b[y, zl, c] = (dot(turned, left64) + dot(placed, right64)).astype(BF)
    fac_z(1)

    @pl.loop(0, NJ)
    def _(j):
        dw_load(j).start()
        dw_send(j).start()

    acc[...] = jnp.zeros_like(acc)
    low[...] = jnp.zeros_like(low)

    def fac_forward(part, yy):
        fac = (fac_a, fac_b)[part]
        return remote(fac.at[yy, :, c], fac.at[yy, :, c],
                      s_fac.at[part, 2], r_facd.at[part, (yy - y + 4) % 4], sibling)

    def fac_y(part):
        fac = (fac_a, fac_b)[part]
        wait_bytes(fac.at[0, pl.ds(0, 3), 0], r_facz.at[part])
        for d in range(3):
            remote(fac.at[y, :, c], fac.at[y, :, c],
                   s_fac.at[part, 1], r_facy.at[part, d], y_peers[d]).start()
        fac_forward(part, y).start()

    def fac_cross(part):
        fac = (fac_a, fac_b)[part]
        for d in range(3):
            wait_bytes(fac.at[0, :, 0], r_facy.at[part, d])
            fac_forward(part, (y + 3 - d) % 4).start()

    def fac_arrive(part):
        for d in range(4):
            fac_forward(part, (y + d) % 4).wait_recv()

    def hidden(om, value):
        high, rest = split(value)
        both = jnp.concatenate([high, rest], axis=1)
        for n in range(2):
            cols, ups = pl.ds(n * 256, 256), pl.ds(HID + n * 256, 256)
            gate = acc[om, :, cols] + dot(both, a2[:, cols])
            up = acc[om, :, ups] + dot(both, a2[:, ups])
            hid[om, c, :, cols] = (gate / (1.0 + jnp.exp(-gate)) * up).astype(BF)
        hid_send(om).start()

    def hid_send(om):
        return remote(hid.at[om, c], hid.at[om, c], s_hid.at[om], r_hid.at[om], sibling)

    def low_down(om):
        hid_send(om).wait_recv()
        value = dot(hid[om, 0], dbf[0]) + dot(hid[om, 1], dbf[1])
        high, rest = split(value)
        low2 = high.astype(F32) + pltpu.roll(rest.astype(F32), 64, 1)
        return low2.astype(BF)

    def down(om, j, low2):
        da = daf[pl.ds(pl.multiple_of(c * HALF + j * JC, JC), JC), :]
        value = dot(hid[om, 0], dw[0, j]) + dot(hid[om, 1], dw[1, j]) + dot_nt(low2, da)
        value = value.astype(BF).reshape(4, 2, CAP, JC)
        back_got[om, j, 0] = value[0]
        back[om, j] = value[1:]
        for d in range(3):
            remote(back.at[om, j, d], back_got.at[om, j, d + 1],
                   s_ret, r_ret.at[om, j], x_down[d]).start()

    def zret(j):
        return remote(zs.at[j], zr.at[j], s_zret.at[j], r_zret.at[j], mirror)

    def combine(om, j):
        wait_bytes(back.at[om, j], r_ret.at[om, j])
        for cs in range(2):
            value = dot(wtab[om, cs], back_got[om, j, :, cs].reshape(4 * CAP, JC))
            value = value[0:ROWS] + value[ROWS:]

            @pl.when(om == 0)
            def _():
                own[j, cs] = value

            @pl.when(om == 1)
            def _():
                zs[j, cs] = value.astype(BF)

        @pl.when(om == 1)
        def _():
            zret(j).start()

    def fin_send(j):
        return remote(fin.at[j], fin_got.at[j], s_fin.at[j], r_fin.at[j], sibling)

    def finish(j):
        zret(j).wait_recv()
        fin[j] = (own[j, 1 - c] + zr[j, 1 - c].astype(F32)).astype(BF)
        fin_send(j).start()
        cols = pl.ds(pl.multiple_of(c * HALF + j * JC, JC), JC)
        out[:, cols] = (own[j, c] + zr[j, c].astype(F32)).astype(BF)

    fac_y(0)

    @pl.loop(0, NK + 1)
    def _(k):
        @pl.when(k < NK)
        def _():
            arrive(0, k)

        @pl.when(k == 3)
        def _():
            meta_mirror.wait_recv()
            meta_second.start()
            make_select(1)

        @pl.when((far == 1) & (k == 4))
        def _():
            fac_y(1)

        @pl.when(k >= 1)
        def _():
            w_load(k - 1, 0).wait()
            w_load(k - 1, 1).wait()
            gate_up(0, k - 1)

        @pl.when((far == 1) & (k >= 4) & (k < NK))
        def _():
            dispatch(1, k - 4)

    @pl.when(far == 0)
    def _():
        @pl.loop(0, 3)
        def _(k):
            dispatch(1, k)

        fac_y(1)

    meta_sibling.wait_recv()
    make_weights(0, 1 - c)
    meta_second.wait_recv()
    make_weights(1, 1 - c)

    @pl.loop(3, NK)
    def _(k):
        dispatch(1, k)
        arrive(1, k - 3)

        @pl.when(k >= 4)
        def _():
            gate_up(1, k - 4)

        @pl.when(k == 4)
        def _():
            fac_cross(0)

    fac_arrive(0)
    for yy in range(4):
        gub[pl.ds(yy * 896, 896), :] = fac_a[yy, :, :, 0:PART, :].reshape(896, 128)
    small = fac_a[:, :, c, PART:PART + 32, :].astype(F32).reshape(16, 4, 8, 128)
    r = iota((128, 128), 0)
    s = iota((128, 128), 1)
    take = onehot((s // 8 == (r % 64) // 4) & (s % 8 == r % 4 + 4 * (r // 64)))
    upper = r < 64
    for q in range(4):
        right = dot(take, small[:, q].reshape(128, 128).astype(BF)).astype(BF)
        none = jnp.zeros_like(right)
        for n in range(2):
            rs = pl.ds(n * 128, 128)
            a2[rs, pl.ds(128 * q, 128)] = jnp.where(upper, right, none)
            a2[rs, pl.ds(HID + 128 * q, 128)] = jnp.where(upper, none, right)
    hidden(0, sum(low_part(0, k) for k in range(NK)))
    fac_cross(1)
    arrive(1, 4)
    gate_up(1, 3)
    fac_arrive(1)
    left = iota((896, 128), 1) < 64
    for yy in range(4):
        part = fac_b[yy].reshape(896, 128).astype(F32)
        part = jnp.where(left, part, 0.0)
        daf[pl.ds(yy * 896, 896), :] = (part + pltpu.roll(part, 64, 1)).astype(BF)
        for core in range(2):
            part = fac_b[yy, :, core, 0:32, :].reshape(128, 128)
            dbf[core, pl.ds(yy * 128, 128), :] = jnp.where(
                iota((128, 128), 1) < 64, jnp.zeros_like(part), part)

    @pl.loop(0, NJ)
    def _(j):
        dw_load(j).wait()
        dw_send(j).wait_recv()

    low_own = low_down(0)
    down(0, 0, low_own)
    arrive(1, 5)
    down(0, 1, low_own)
    gate_up(1, 4)
    low[...] = sum(low_part(1, k) for k in range(5))
    arrive(1, 6)
    down(0, 2, low_own)
    gate_up(1, 5)
    gate_up(1, 6)
    hidden(1, low[...] + low_part(1, 5) + low_part(1, 6))
    low_mirror = low_down(1)

    @pl.loop(0, NJ)
    def _(j):
        down(1, j, low_mirror)

    @pl.loop(3, NJ)
    def _(j):
        down(0, j, low_own)

    @pl.loop(0, NJ)
    def _(j):
        combine(1, j)

    @pl.loop(0, NJ)
    def _(j):
        combine(0, j)
        finish(j)

    @pl.loop(0, NJ)
    def _(j):
        fin_send(j).wait_recv()
        cols = pl.ds(pl.multiple_of((1 - c) * HALF + j * JC, JC), JC)
        out[:, cols] = fin_got[j]

    meta_mirror.wait_send()
    meta_sibling.wait_send()
    meta_second.wait_send()
    wait_bytes(sel, s_x)
    wait_bytes(back, s_ret)
    for part, fac in enumerate((fac_a, fac_b)):
        wait_bytes(fac.at[0, pl.ds(0, 3), 0], s_fac.at[part, 0])
        wait_bytes(fac.at[pl.ds(0, 3), :, 0], s_fac.at[part, 1])
        wait_bytes(fac.at[:, :, 0], s_fac.at[part, 2])
    for om in range(2):
        hid_send(om).wait_send()

        @pl.loop(0, NK)
        def _(k):
            forward(om, k).wait_send()

    @pl.loop(0, NJ)
    def _(j):
        zrow(j).wait_send()
        dw_send(j).wait_send()
        zret(j).wait_send()
        fin_send(j).wait_send()


def on_device(rows, ids, wts, gate_w, up_w, down_w, gate_b, gate_a, up_b, up_a, down_b, down_a):
    args = (rows, ids.T, wts.T, gate_w, up_w, down_w, gate_b.swapaxes(1, 2), gate_a,
            up_b.swapaxes(1, 2), up_a, down_b, down_a)
    vmem = pl.BlockSpec(memory_space=pltpu.VMEM)
    hbm = pl.BlockSpec(memory_space=pltpu.HBM)
    dma = pltpu.SemaphoreType.DMA
    scratch = [
        pltpu.VMEM((2, NK, ROWS, KC), BF),
        pltpu.VMEM((2, 2, ROWS, 128), F32),
        pltpu.VMEM((2, 128, ROWS), BF),
        pltpu.VMEM((2, 2, 2 * ROWS, 128), BF),
        pltpu.VMEM((2, NK, 3, CAP, KC), BF),
        pltpu.VMEM((2, NK, 4, 2, CAP, KC), BF),
        pltpu.VMEM((NK, KC, 2 * HID), BF),
        pltpu.VMEM((2, NJ, HID, JC), BF),
        pltpu.VMEM((2, 8 * CAP, 2 * HID), F32),
        pltpu.VMEM((8 * CAP, 128), F32),
        pltpu.VMEM((2, 2, 8 * CAP, HID), BF),
        pltpu.VMEM((2, NJ, 3, 2, CAP, JC), BF),
        pltpu.VMEM((2, NJ, 4, 2, CAP, JC), BF),
        pltpu.VMEM((2, ROWS), jnp.int32),
        pltpu.VMEM((2, ROWS), F32),
        pltpu.VMEM((1, 4, HID), BF),
        pltpu.VMEM((1, 4, HID), BF),
        pltpu.VMEM((1, 32, RANK), BF),
        pltpu.VMEM((RANK, SHARD), BF),
        pltpu.VMEM((RANK, SHARD), BF),
        pltpu.VMEM((RANK, SHARD), BF),
        pltpu.VMEM((4, 4, 2, PART + 32, 128), BF),
        pltpu.VMEM((4, 4, 2, PART, 128), BF),
        pltpu.VMEM((D, 128), BF),
        pltpu.VMEM((D, 128), BF),
        pltpu.VMEM((2, HID, 128), BF),
        pltpu.VMEM((256, 2 * HID), BF),
        pltpu.VMEM((NJ, 2, ROWS, JC), BF),
        pltpu.VMEM((NJ, 2, ROWS, JC), BF),
        pltpu.VMEM((NJ, 2, ROWS, JC), F32),
        pltpu.VMEM((NJ, ROWS, JC), BF),
        pltpu.VMEM((NJ, ROWS, JC), BF),
        dma((NK + 8,)),
        dma((NK, 2)),
        dma((NJ,)),
        dma((3,)),
        dma((NK,)),
        dma((NK,)),
        dma((3,)),
        dma,
        dma((2, NK)),
        dma((2, NK)),
        dma((2, NK)),
        dma((NJ,)),
        dma((NJ,)),
        dma((2, 3)),
        dma((2,)),
        dma((2, 3)),
        dma((2, 4)),
        dma((2,)),
        dma((2,)),
        dma,
        dma((2, NJ)),
        dma((NJ,)),
        dma((NJ,)),
        dma((NJ,)),
        dma((NJ,)),
    ]
    return pl.pallas_call(
        kernel,
        out_shape=jax.ShapeDtypeStruct((ROWS, D), BF),
        in_specs=[hbm] * 12,
        out_specs=vmem,
        scratch_shapes=scratch,
        compiler_params=pltpu.CompilerParams(
            collective_id=0, has_side_effects=True, vmem_limit_bytes=63 << 20),
        cost_estimate=pl.CostEstimate(
            flops=8 << 30, bytes_accessed=13 << 20, transcendentals=1 << 18),
        name="expert_layer",
    )(*args)


def solution(mesh):
    return jax.shard_map(
        on_device,
        mesh=mesh,
        in_specs=(
            P(("group", "expert"), None),
            P(("group", "expert"), None),
            P(("group", "expert"), None),
            P("expert", None, None),
            P("expert", None, None),
            P("expert", None, None),
            P(None, "group", None),
            P("expert", "group", None),
            P(None, "group", None),
            P("expert", "group", None),
            P("expert", "group", None),
            P(None, None, "group"),
        ),
        out_specs=P(("group", "expert"), None),
        check_vma=False,
    )
```

```python
import jax
import jax.numpy as jnp
from jax import lax
from jax.experimental import pallas as pl
from jax.experimental.pallas import tpu as pltpu
from jax.sharding import PartitionSpec as P

MESH = pl.DeviceIdType.MESH
BF = jnp.bfloat16
F32 = jnp.float32

D = 3584
HID = 512
ROWS = 64
CAP = 32
RANK = 64
KC = 512
NK = D // KC
HALF = D // 2
JC = 256
NJ = HALF // JC
SHARD = 224
PART = SHARD // 2


def iota(shape, dim):
    return lax.broadcasted_iota(jnp.int32, shape, dim)


def onehot(mask):
    return jnp.where(mask, 1.0, 0.0).astype(BF)


def dot(a, b):
    return jnp.dot(a, b, preferred_element_type=F32)


def dot_nt(a, b):
    return lax.dot_general(a, b, (((1,), (1,)), ((), ())), preferred_element_type=F32)


def split(v):
    high = v.astype(BF)
    return high, (v - high.astype(F32)).astype(BF)


def kernel(
    rows, ids, wts, gate_w, up_w, down_w, gate_b, gate_a, up_b, up_a, down_b, down_a,
    out,
    rw, meta, tab, wtab, sel, got, w, dw, acc, hid, back, back_got,
    ids_v, wts_v, ga_v, ua_v, db_v, pack_g, pack_u, pack_d, fac_a, fac_b, gub, daf, dbf, a2,
    zs, zr, own, fin, fin_got,
    s_load, s_w, s_dw, s_meta, s_zrow, r_zrow, r_meta,
    s_x, r_x, s_fwd, r_fwd, s_dwx, r_dwx, s_fac, r_facz, r_facy, r_facd,
    s_hid, r_hid, s_ret, r_ret, s_zret, r_zret, s_fin, r_fin,
):
    g = lax.axis_index("group")
    e = lax.axis_index("expert")
    y, zl = g // 4, g % 4
    x, zh, c = e // 4, (e // 2) % 2, e % 2
    pair = e // 2

    def dev(y_, zl_, x_, zh_, c_):
        return (y_ * 4 + zl_, (x_ * 2 + zh_) * 2 + c_)

    sibling = dev(y, zl, x, zh, 1 - c)
    mirror = dev(y, 3 - zl, x, 1 - zh, c)
    x_up = [dev(y, zl, (x + d) % 4, zh, c) for d in (1, 2, 3)]
    x_down = [dev(y, zl, (x + 4 - d) % 4, zh, c) for d in (1, 2, 3)]
    z_peers = [dev(y, (zl + d) % 4, x, zh, c) for d in (1, 2, 3)]
    y_peers = [dev((y + d) % 4, zl, x, zh, c) for d in (1, 2, 3)]
    far = jnp.where((zl == 1) | (zl == 2), 1, 0)

    def remote(src, dst, ssem, rsem, target):
        return pltpu.make_async_remote_copy(
            src_ref=src, dst_ref=dst, send_sem=ssem, recv_sem=rsem,
            device_id=target, device_id_type=MESH)

    def wait_bytes(ref, sem):
        pltpu.make_async_copy(ref, ref, sem).wait()

    loads = [
        pltpu.make_async_copy(src, dst, s_load.at[NK + n]) for n, (src, dst) in enumerate((
            (ids, ids_v), (wts, wts_v), (gate_b.at[pair], pack_g), (up_b.at[pair], pack_u),
            (down_a.at[pair], pack_d), (gate_a, ga_v), (up_a, ua_v), (down_b, db_v)))
    ]
    for copy in loads:
        copy.start()

    def row_load(k):
        return pltpu.make_async_copy(
            rows.at[:, pl.ds(pl.multiple_of(k * KC, KC), KC)], rw.at[0, k], s_load.at[k])

    def w_load(k, part):
        src = (gate_w, up_w)[part]
        return pltpu.make_async_copy(
            src.at[0, pl.ds(pl.multiple_of(k * KC, KC), KC), :],
            w.at[k, :, pl.ds(part * HID, HID)], s_w.at[k, part])

    def dw_cols(core, j):
        return down_w.at[0, :, pl.ds(pl.multiple_of(core * HALF + j * JC, JC), JC)]

    def dw_load(j):
        return pltpu.make_async_copy(dw_cols(c, j), dw.at[c, j], s_dw.at[j])

    def dw_send(j):
        return remote(dw_cols(1 - c, j), dw.at[c, j], s_dwx.at[j], r_dwx.at[j], sibling)

    @pl.loop(0, NK)
    def _(k):
        row_load(k).start()

    @pl.loop(0, NK)
    def _(k):
        w_load(k, 0).start()
        w_load(k, 1).start()

    barrier = pltpu.get_barrier_semaphore()
    peers = [sibling, mirror] + x_up + z_peers + y_peers
    for peer in peers:
        pl.semaphore_signal(barrier, inc=1, device_id=peer, device_id_type=MESH)

    loads[0].wait()
    loads[1].wait()
    line = iota((128, ROWS), 0)
    idf = ids_v[...].astype(F32)
    named = jnp.where(
        line == 0, idf[0:1, :],
        jnp.where(line == 1, idf[1:2, :], jnp.where(line == 2, wts_v[0:1, :], wts_v[1:2, :])))
    meta[0, c] = named.T

    pl.semaphore_wait(barrier, len(peers))

    meta_mirror = remote(meta.at[0, c], meta.at[1, c], s_meta.at[0], r_meta.at[0], mirror)
    meta_sibling = remote(meta.at[0, c], meta.at[0, c], s_meta.at[1], r_meta.at[1], sibling)
    meta_second = remote(meta.at[1, c], meta.at[1, c], s_meta.at[2], r_meta.at[2], sibling)
    meta_mirror.start()
    meta_sibling.start()

    def zrow(k):
        return remote(
            rows.at[:, pl.ds(pl.multiple_of(k * KC, KC), KC)], rw.at[1, k],
            s_zrow.at[k], r_zrow.at[k], mirror)

    def tables(m):
        lane = iota((ROWS, 128), 1)
        expert = (((x + lane // 32) % 4) * 2 + zh).astype(F32)
        hit0, hit1 = m[:, 0:1] == expert, m[:, 1:2] == expert
        hit = jnp.where(hit0, 1.0, 0.0) + jnp.where(hit1, 1.0, 0.0)
        before = onehot(iota((ROWS, ROWS), 1) < iota((ROWS, ROWS), 0))
        place = dot(before, hit.astype(BF))
        table = jnp.where(place == (lane % 32).astype(F32), hit, 0.0)
        weight = jnp.where(hit0, m[:, 2:3], 0.0) + jnp.where(hit1, m[:, 3:4], 0.0)
        return table, table * weight

    def make_select(om):
        table, weight = tables(meta[om, c])
        tab[om] = table.T.astype(BF)
        high, rest = split(weight)
        wtab[om, c, 0:ROWS, :] = high
        wtab[om, c, ROWS:2 * ROWS, :] = rest

    def make_weights(om, cs):
        _, weight = tables(meta[om, cs])
        high, rest = split(weight)
        wtab[om, cs, 0:ROWS, :] = high
        wtab[om, cs, ROWS:2 * ROWS, :] = rest

    def dispatch(om, k):
        @pl.when(om == 0)
        def _():
            row_load(k).wait()

        @pl.when(om == 1)
        def _():
            zrow(k).wait_recv()

        value = dot(tab[om], rw[om, k]).astype(BF)
        got[om, k, 0, c] = value[0:CAP]
        sel[om, k] = value[CAP:].reshape(3, CAP, KC)
        for d in range(3):
            remote(sel.at[om, k, d], got.at[om, k, d + 1, c], s_x, r_x.at[om, k], x_up[d]).start()

    def forward(om, k):
        return remote(got.at[om, k, :, c], got.at[om, k, :, c],
                      s_fwd.at[om, k], r_fwd.at[om, k], sibling)

    def arrive(om, k):
        wait_bytes(sel.at[om, k], r_x.at[om, k])
        forward(om, k).start()

    def span(st):
        return pl.ds(0, 8 * CAP) if st == 0 else pl.ds((st - 1) * 4 * CAP, 4 * CAP)

    def chosen(st, k):
        if st == 0:
            return got[0, k].reshape(8 * CAP, KC)
        return got[1, k, :, st - 1].reshape(4 * CAP, KC)

    def gate_up(st, k):
        om, rs = min(st, 1), span(st)
        if st == 0:
            forward(0, k).wait_recv()
        else:
            @pl.when(c == 2 - st)
            def _():
                forward(1, k).wait_recv()
        value = chosen(st, k)
        for n in range(4):
            cols = pl.ds(n * 256, 256)
            acc[om, rs, cols] += dot(value, w[k, :, cols])

    def low_rank(st):
        return sum(dot(chosen(st, k), gub[pl.ds(k * KC, KC), :]) for k in range(NK))

    def zrow_start():
        @pl.loop(0, NK)
        def _(k):
            zrow(k).start()

    @pl.when((far == 0) & (c == 0))
    def _():
        zrow_start()

    for copy in loads[2:]:
        copy.wait()
    left64 = onehot(iota((64, 128), 0) == iota((64, 128), 1))
    right64 = onehot(iota((64, 128), 0) + 64 == iota((64, 128), 1))
    pick = onehot(iota((PART, SHARD), 1) == iota((PART, SHARD), 0) + c * PART)
    fac_a[y, zl, c, 0:PART, :] = (
        dot(dot_nt(pick, pack_g[...]).astype(BF), left64)
        + dot(dot_nt(pick, pack_u[...]).astype(BF), right64)).astype(BF)
    rights = jnp.concatenate([ga_v[0].astype(F32), ua_v[0].astype(F32)], axis=0)
    fac_a[y, zl, c, PART:PART + 32, :] = jnp.concatenate(
        [rights[:, 128 * q:128 * q + 128] for q in range(4)], axis=0).astype(BF)

    def fac_y_send(part, zz):
        fac = (fac_a, fac_b)[part]
        for d in range(3):
            remote(fac.at[y, zz, c], fac.at[y, zz, c],
                   s_fac.at[part, 1], r_facy.at[part, d], y_peers[d]).start()

    def fac_z(part):
        fac = (fac_a, fac_b)[part]
        for d in range(3):
            remote(fac.at[y, zl, c], fac.at[y, zl, c],
                   s_fac.at[part, 0], r_facz.at[part, d], z_peers[d]).start()
        fac_y_send(part, zl)

    fac_z(0)

    @pl.when((far == 1) & (c == 0))
    def _():
        zrow_start()

    make_select(0)

    @pl.loop(0, NK)
    def _(k):
        dispatch(0, k)

    turned = dot_nt(pick, pack_d[...]).astype(BF)
    placed = dot(onehot(iota((PART, 32), 0) == iota((PART, 32), 1)), db_v[0]).astype(BF)
    fac_b[y, zl, c] = (dot(turned, left64) + dot(placed, right64)).astype(BF)
    fac_z(1)

    @pl.loop(0, NJ)
    def _(j):
        dw_load(j).start()
        dw_send(j).start()

    acc[...] = jnp.zeros_like(acc)

    def fac_forward(part, yy):
        fac = (fac_a, fac_b)[part]
        return remote(fac.at[yy, :, c], fac.at[yy, :, c],
                      s_fac.at[part, 2], r_facd.at[part, (yy - y + 4) % 4], sibling)

    def fac_y(part):
        fac = (fac_a, fac_b)[part]
        for d in range(3):
            wait_bytes(fac.at[0, 0, 0], r_facz.at[part, d])
            fac_y_send(part, (zl + 3 - d) % 4)
        fac_forward(part, y).start()

    def fac_cross(part):
        fac = (fac_a, fac_b)[part]
        for d in range(3):
            wait_bytes(fac.at[0, :, 0], r_facy.at[part, d])
            fac_forward(part, (y + 3 - d) % 4).start()

    def fac_arrive(part):
        for d in range(4):
            fac_forward(part, (y + d) % 4).wait_recv()

    def hidden(st):
        om, rs = min(st, 1), span(st)
        high, rest = split(low_rank(st))
        both = jnp.concatenate([high, rest], axis=1)
        for n in range(2):
            cols, ups = pl.ds(n * 256, 256), pl.ds(HID + n * 256, 256)
            gate = acc[om, rs, cols] + dot(both, a2[:, cols])
            up = acc[om, rs, ups] + dot(both, a2[:, ups])
            hid[om, c, rs, cols] = (gate / (1.0 + jnp.exp(-gate)) * up).astype(BF)
        hid_send(st).start()

    def hid_send(st):
        part = hid.at[min(st, 1), c, span(st)]
        return remote(part, part, s_hid.at[st], r_hid.at[st], sibling)

    def low_down(st):
        om, rs = min(st, 1), span(st)
        hid_send(st).wait_recv()
        value = dot(hid[om, 0, rs], dbf[0]) + dot(hid[om, 1, rs], dbf[1])
        high, rest = split(value)
        low2 = high.astype(F32) + pltpu.roll(rest.astype(F32), 64, 1)
        return low2.astype(BF)

    def down(st, j, low2):
        om, rs = min(st, 1), span(st)
        da = daf[pl.ds(pl.multiple_of(c * HALF + j * JC, JC), JC), :]
        value = dot(hid[om, 0, rs], dw[0, j]) + dot(hid[om, 1, rs], dw[1, j]) + dot_nt(low2, da)
        value = value.astype(BF)
        if st == 0:
            value = value.reshape(4, 2, CAP, JC)
            back_got[0, j, 0] = value[0]
            back[0, j] = value[1:]
        else:
            value = value.reshape(4, CAP, JC)
            back_got[1, j, 0, st - 1] = value[0]
            back[1, j, :, st - 1] = value[1:]
        for d in range(3):
            if st == 0:
                src, dst = back.at[0, j, d], back_got.at[0, j, d + 1]
            else:
                src, dst = back.at[1, j, d, st - 1], back_got.at[1, j, d + 1, st - 1]
            remote(src, dst, s_ret, r_ret.at[st, j], x_down[d]).start()

    def zret(m, j):
        return remote(zs.at[j, m], zr.at[j, m], s_zret.at[m, j], r_zret.at[m, j], mirror)

    def mix(om, cs, j):
        value = dot(wtab[om, cs], back_got[om, j, :, cs].reshape(4 * CAP, JC))
        return value[0:ROWS] + value[ROWS:]

    def combine(st, j):
        if st == 0:
            wait_bytes(back.at[0, j], r_ret.at[0, j])
            for cs in range(2):
                own[j, cs] = mix(0, cs, j)
        else:
            wait_bytes(back.at[1, j, :, st - 1], r_ret.at[st, j])
            zs[j, st - 1] = mix(1, st - 1, j).astype(BF)
            zret(st - 1, j).start()

    def fin_send(j):
        return remote(fin.at[j], fin_got.at[j], s_fin.at[j], r_fin.at[j], sibling)

    def finish(j):
        zret(0, j).wait_recv()
        zret(1, j).wait_recv()
        fin[j] = (own[j, 1 - c] + zr[j, 1 - c].astype(F32)).astype(BF)
        fin_send(j).start()
        cols = pl.ds(pl.multiple_of(c * HALF + j * JC, JC), JC)
        out[:, cols] = (own[j, c] + zr[j, c].astype(F32)).astype(BF)

    fac_y(0)

    @pl.loop(0, NK + 2)
    def _(k):
        @pl.when(k < NK)
        def _():
            arrive(0, k)

        @pl.when(((far == 1) & (c == 1) & (k == 4)) | ((far == 0) & (c == 1) & (k == 6)))
        def _():
            zrow_start()

        @pl.when(k == 3)
        def _():
            meta_mirror.wait_recv()
            meta_second.start()
            make_select(1)

        @pl.when((far == 1) & (k == 3))
        def _():
            fac_y(1)

        @pl.when((far == 1) & (c == 0) & (k >= 3) & (k < NK))
        def _():
            dispatch(1, 2 * k - 6)

            @pl.when(k < NK - 1)
            def _():
                dispatch(1, 2 * k - 5)

        @pl.when(k >= 2)
        def _():
            w_load(k - 2, 0).wait()
            w_load(k - 2, 1).wait()
            gate_up(0, k - 2)

    fac_cross(0)

    @pl.when(far == 0)
    def _():
        fac_y(1)

    @pl.when((far == 0) & (c == 0))
    def _():
        @pl.loop(0, NK)
        def _(k):
            dispatch(1, k)

    meta_sibling.wait_recv()
    make_weights(0, 1 - c)
    meta_second.wait_recv()
    make_weights(1, 1 - c)

    @pl.when((far == 1) & (c == 1))
    def _():
        @pl.loop(0, 4)
        def _(k):
            dispatch(1, k)

    fac_arrive(0)
    for yy in range(4):
        gub[pl.ds(yy * 896, 896), :] = fac_a[yy, :, :, 0:PART, :].reshape(896, 128)
    small = fac_a[:, :, c, PART:PART + 32, :].astype(F32).reshape(16, 4, 8, 128)
    r = iota((128, 128), 0)
    s = iota((128, 128), 1)
    take = onehot((s // 8 == (r % 64) // 4) & (s % 8 == r % 4 + 4 * (r // 64)))
    upper = r < 64
    for q in range(4):
        right = dot(take, small[:, q].reshape(128, 128).astype(BF)).astype(BF)
        none = jnp.zeros_like(right)
        for n in range(2):
            rs = pl.ds(n * 128, 128)
            a2[rs, pl.ds(128 * q, 128)] = jnp.where(upper, right, none)
            a2[rs, pl.ds(HID + 128 * q, 128)] = jnp.where(upper, none, right)
    @pl.when(far == 0)
    def _():
        hidden(0)

    @pl.when((far == 1) & (c == 1))
    def _():
        @pl.loop(4, NK)
        def _(k):
            dispatch(1, k)

    @pl.loop(0, NK + 1)
    def _(k):
        @pl.when((c == 0) & (k < NK))
        def _():
            arrive(1, k)

        @pl.when((far == 0) & (c == 1) & (k < NK))
        def _():
            dispatch(1, k)

        @pl.when(k == 5)
        def _():
            fac_cross(1)

        @pl.when(k > 0)
        def _():
            gate_up(1, k - 1)

    hidden(1)

    @pl.when(far == 1)
    def _():
        hidden(0)

    fac_arrive(1)
    left = iota((896, 128), 1) < 64
    for yy in range(4):
        part = fac_b[yy].reshape(896, 128).astype(F32)
        part = jnp.where(left, part, 0.0)
        daf[pl.ds(yy * 896, 896), :] = (part + pltpu.roll(part, 64, 1)).astype(BF)
        for core in range(2):
            part = fac_b[yy, :, core, 0:32, :].reshape(128, 128)
            dbf[core, pl.ds(yy * 128, 128), :] = jnp.where(
                iota((128, 128), 1) < 64, jnp.zeros_like(part), part)


    @pl.loop(0, NJ)
    def _(j):
        dw_load(j).wait()
        dw_send(j).wait_recv()

    low_a = low_down(1)

    @pl.loop(0, NJ)
    def _(j):
        down(1, j, low_a)

    low_own = low_down(0)
    down(0, 0, low_own)
    down(0, 1, low_own)

    @pl.when(far == 1)
    def _():
        @pl.when(c == 1)
        def _():
            @pl.loop(0, NK)
            def _(k):
                arrive(1, k)

        combine(1, 0)
        combine(1, 1)

        @pl.loop(0, NK)
        def _(k):
            @pl.when(c == 0)
            def _():
                forward(1, k).wait_recv()

        rs = span(2)
        for n in range(4):
            cols = pl.ds(n * 256, 256)
            acc[1, rs, cols] = sum(dot(chosen(2, k), w[k, :, cols]) for k in range(NK))

    @pl.when(far == 0)
    def _():
        @pl.loop(0, NK + 1)
        def _(k):
            @pl.when((c == 1) & (k < NK))
            def _():
                arrive(1, k)

            @pl.when(k > 0)
            def _():
                gate_up(2, k - 1)

            @pl.when(k >= NK - 1)
            def _():
                combine(1, k - NK + 1)

    hidden(2)
    combine(1, 2)
    low_b = low_down(2)

    @pl.loop(0, NJ)
    def _(j):
        down(2, j, low_b)

        @pl.when(j < NJ - 3)
        def _():
            combine(1, j + 3)

    @pl.loop(2, NJ)
    def _(j):
        down(0, j, low_own)

    @pl.loop(0, NJ)
    def _(j):
        combine(2, j)

    @pl.loop(0, NJ)
    def _(j):
        combine(0, j)
        finish(j)

    @pl.loop(0, NJ)
    def _(j):
        fin_send(j).wait_recv()
        cols = pl.ds(pl.multiple_of((1 - c) * HALF + j * JC, JC), JC)
        out[:, cols] = fin_got[j]

    meta_mirror.wait_send()
    meta_sibling.wait_send()
    meta_second.wait_send()
    wait_bytes(sel, s_x)
    wait_bytes(back, s_ret)
    for part, fac in enumerate((fac_a, fac_b)):
        wait_bytes(fac.at[0, pl.ds(0, 3), 0], s_fac.at[part, 0])
        wait_bytes(fac.at[pl.ds(0, 3), :, 0], s_fac.at[part, 1])
        wait_bytes(fac.at[:, :, 0], s_fac.at[part, 2])
    for st in range(3):
        hid_send(st).wait_send()
    for om in range(2):

        @pl.loop(0, NK)
        def _(k):
            forward(om, k).wait_send()

    @pl.loop(0, NJ)
    def _(j):
        zrow(j).wait_send()
        dw_send(j).wait_send()
        zret(0, j).wait_send()
        zret(1, j).wait_send()
        fin_send(j).wait_send()


def on_device(rows, ids, wts, gate_w, up_w, down_w, gate_b, gate_a, up_b, up_a, down_b, down_a):
    args = (rows, ids.T, wts.T, gate_w, up_w, down_w, gate_b.swapaxes(1, 2), gate_a,
            up_b.swapaxes(1, 2), up_a, down_b, down_a)
    vmem = pl.BlockSpec(memory_space=pltpu.VMEM)
    hbm = pl.BlockSpec(memory_space=pltpu.HBM)
    dma = pltpu.SemaphoreType.DMA
    scratch = [
        pltpu.VMEM((2, NK, ROWS, KC), BF),
        pltpu.VMEM((2, 2, ROWS, 128), F32),
        pltpu.VMEM((2, 128, ROWS), BF),
        pltpu.VMEM((2, 2, 2 * ROWS, 128), BF),
        pltpu.VMEM((2, NK, 3, CAP, KC), BF),
        pltpu.VMEM((2, NK, 4, 2, CAP, KC), BF),
        pltpu.VMEM((NK, KC, 2 * HID), BF),
        pltpu.VMEM((2, NJ, HID, JC), BF),
        pltpu.VMEM((2, 8 * CAP, 2 * HID), F32),
        pltpu.VMEM((2, 2, 8 * CAP, HID), BF),
        pltpu.VMEM((2, NJ, 3, 2, CAP, JC), BF),
        pltpu.VMEM((2, NJ, 4, 2, CAP, JC), BF),
        pltpu.VMEM((2, ROWS), jnp.int32),
        pltpu.VMEM((2, ROWS), F32),
        pltpu.VMEM((1, 4, HID), BF),
        pltpu.VMEM((1, 4, HID), BF),
        pltpu.VMEM((1, 32, RANK), BF),
        pltpu.VMEM((RANK, SHARD), BF),
        pltpu.VMEM((RANK, SHARD), BF),
        pltpu.VMEM((RANK, SHARD), BF),
        pltpu.VMEM((4, 4, 2, PART + 32, 128), BF),
        pltpu.VMEM((4, 4, 2, PART, 128), BF),
        pltpu.VMEM((D, 128), BF),
        pltpu.VMEM((D, 128), BF),
        pltpu.VMEM((2, HID, 128), BF),
        pltpu.VMEM((256, 2 * HID), BF),
        pltpu.VMEM((NJ, 2, ROWS, JC), BF),
        pltpu.VMEM((NJ, 2, ROWS, JC), BF),
        pltpu.VMEM((NJ, 2, ROWS, JC), F32),
        pltpu.VMEM((NJ, ROWS, JC), BF),
        pltpu.VMEM((NJ, ROWS, JC), BF),
        dma((NK + 8,)),
        dma((NK, 2)),
        dma((NJ,)),
        dma((3,)),
        dma((NK,)),
        dma((NK,)),
        dma((3,)),
        dma,
        dma((2, NK)),
        dma((2, NK)),
        dma((2, NK)),
        dma((NJ,)),
        dma((NJ,)),
        dma((2, 3)),
        dma((2, 3)),
        dma((2, 3)),
        dma((2, 4)),
        dma((3,)),
        dma((3,)),
        dma,
        dma((3, NJ)),
        dma((2, NJ)),
        dma((2, NJ)),
        dma((NJ,)),
        dma((NJ,)),
    ]
    return pl.pallas_call(
        kernel,
        out_shape=jax.ShapeDtypeStruct((ROWS, D), BF),
        in_specs=[hbm] * 12,
        out_specs=vmem,
        scratch_shapes=scratch,
        compiler_params=pltpu.CompilerParams(
            collective_id=0, has_side_effects=True, vmem_limit_bytes=63 << 20),
        cost_estimate=pl.CostEstimate(
            flops=8 << 30, bytes_accessed=13 << 20, transcendentals=1 << 18),
        name="expert_layer",
    )(*args)


def solution(mesh):
    return jax.shard_map(
        on_device,
        mesh=mesh,
        in_specs=(
            P(("group", "expert"), None),
            P(("group", "expert"), None),
            P(("group", "expert"), None),
            P("expert", None, None),
            P("expert", None, None),
            P("expert", None, None),
            P(None, "group", None),
            P("expert", "group", None),
            P(None, "group", None),
            P("expert", "group", None),
            P("expert", "group", None),
            P(None, None, "group"),
        ),
        out_specs=P(("group", "expert"), None),
        check_vma=False,
    )
```

```python
import jax
import jax.numpy as jnp
from jax import lax
from jax.experimental import pallas as pl
from jax.experimental.pallas import tpu as pltpu
from jax.sharding import PartitionSpec as P

MESH = pl.DeviceIdType.MESH
BF = jnp.bfloat16
F32 = jnp.float32

D = 3584
HID = 512
ROWS = 64
CAP = 32
RANK = 64
KC = 512
NK = D // KC
HALF = D // 2
JC = 256
NJ = HALF // JC
SHARD = 224
PART = SHARD // 2


def iota(shape, dim):
    return lax.broadcasted_iota(jnp.int32, shape, dim)


def onehot(mask):
    return jnp.where(mask, 1.0, 0.0).astype(BF)


def dot(a, b):
    return jnp.dot(a, b, preferred_element_type=F32)


def dot_nt(a, b):
    return lax.dot_general(a, b, (((1,), (1,)), ((), ())), preferred_element_type=F32)


def split(v):
    high = v.astype(BF)
    return high, (v - high.astype(F32)).astype(BF)


def kernel(
    rows, ids, wts, gate_w, up_w, down_w, gate_b, gate_a, up_b, up_a, down_b, down_a,
    out,
    rw, meta, tab, wtab, sel, got, w, dw, acc, hid, back, back_got,
    ids_v, wts_v, ga_v, ua_v, db_v, pack_g, pack_u, pack_d, fac_a, fac_b, gub, daf, dbf, a2,
    zs, zr, own, fin, fin_got,
    s_load, s_w, s_dw, s_meta, s_zrow, r_zrow, r_meta,
    s_x, r_x, s_fwd, r_fwd, s_dwx, r_dwx, s_fac, r_facz, r_facy, r_facd,
    s_hid, r_hid, s_ret, r_ret, s_zret, r_zret, s_fin, r_fin,
):
    g = lax.axis_index("group")
    e = lax.axis_index("expert")
    y, zl = g // 4, g % 4
    x, zh, c = e // 4, (e // 2) % 2, e % 2
    pair = e // 2

    def dev(y_, zl_, x_, zh_, c_):
        return (y_ * 4 + zl_, (x_ * 2 + zh_) * 2 + c_)

    sibling = dev(y, zl, x, zh, 1 - c)
    mirror = dev(y, 3 - zl, x, 1 - zh, c)
    x_up = [dev(y, zl, (x + d) % 4, zh, c) for d in (1, 2, 3)]
    x_down = [dev(y, zl, (x + 4 - d) % 4, zh, c) for d in (1, 2, 3)]
    z_peers = [dev(y, (zl + d) % 4, x, zh, c) for d in (1, 2, 3)]
    y_peers = [dev((y + d) % 4, zl, x, zh, c) for d in (1, 2, 3)]
    far = jnp.where((zl == 1) | (zl == 2), 1, 0)

    def remote(src, dst, ssem, rsem, target):
        return pltpu.make_async_remote_copy(
            src_ref=src, dst_ref=dst, send_sem=ssem, recv_sem=rsem,
            device_id=target, device_id_type=MESH)

    def wait_bytes(ref, sem):
        pltpu.make_async_copy(ref, ref, sem).wait()

    loads = [
        pltpu.make_async_copy(src, dst, s_load.at[NK + n]) for n, (src, dst) in enumerate((
            (ids, ids_v), (wts, wts_v), (gate_b.at[pair], pack_g), (up_b.at[pair], pack_u),
            (down_a.at[pair], pack_d), (gate_a, ga_v), (up_a, ua_v), (down_b, db_v)))
    ]
    for copy in loads:
        copy.start()

    def row_load(k):
        return pltpu.make_async_copy(
            rows.at[:, pl.ds(pl.multiple_of(k * KC, KC), KC)], rw.at[0, k], s_load.at[k])

    def w_load(k, part):
        src = (gate_w, up_w)[part]
        return pltpu.make_async_copy(
            src.at[0, pl.ds(pl.multiple_of(k * KC, KC), KC), :],
            w.at[k, :, pl.ds(part * HID, HID)], s_w.at[k, part])

    def dw_cols(core, j):
        return down_w.at[0, :, pl.ds(pl.multiple_of(core * HALF + j * JC, JC), JC)]

    def dw_load(j):
        return pltpu.make_async_copy(dw_cols(c, j), dw.at[c, j], s_dw.at[j])

    def dw_send(j):
        return remote(dw_cols(1 - c, j), dw.at[c, j], s_dwx.at[j], r_dwx.at[j], sibling)

    @pl.loop(0, NK)
    def _(k):
        row_load(k).start()

    @pl.loop(0, NK)
    def _(k):
        w_load(k, 0).start()
        w_load(k, 1).start()

    barrier = pltpu.get_barrier_semaphore()
    peers = [sibling, mirror] + x_up + z_peers + y_peers
    for peer in peers:
        pl.semaphore_signal(barrier, inc=1, device_id=peer, device_id_type=MESH)

    loads[0].wait()
    loads[1].wait()
    line = iota((128, ROWS), 0)
    idf = ids_v[...].astype(F32)
    named = jnp.where(
        line == 0, idf[0:1, :],
        jnp.where(line == 1, idf[1:2, :], jnp.where(line == 2, wts_v[0:1, :], wts_v[1:2, :])))
    meta[0, c] = named.T

    pl.semaphore_wait(barrier, len(peers))

    meta_mirror = remote(meta.at[0, c], meta.at[1, c], s_meta.at[0], r_meta.at[0], mirror)
    meta_sibling = remote(meta.at[0, c], meta.at[0, c], s_meta.at[1], r_meta.at[1], sibling)
    meta_second = remote(meta.at[1, c], meta.at[1, c], s_meta.at[2], r_meta.at[2], sibling)
    meta_mirror.start()
    meta_sibling.start()

    def zrow(k):
        return remote(
            rows.at[:, pl.ds(pl.multiple_of(k * KC, KC), KC)], rw.at[1, k],
            s_zrow.at[k], r_zrow.at[k], mirror)

    def tables(m):
        lane = iota((ROWS, 128), 1)
        expert = (((x + lane // 32) % 4) * 2 + zh).astype(F32)
        hit0, hit1 = m[:, 0:1] == expert, m[:, 1:2] == expert
        hit = jnp.where(hit0, 1.0, 0.0) + jnp.where(hit1, 1.0, 0.0)
        before = onehot(iota((ROWS, ROWS), 1) < iota((ROWS, ROWS), 0))
        place = dot(before, hit.astype(BF))
        table = jnp.where(place == (lane % 32).astype(F32), hit, 0.0)
        weight = jnp.where(hit0, m[:, 2:3], 0.0) + jnp.where(hit1, m[:, 3:4], 0.0)
        return table, table * weight

    def make_select(om):
        table, weight = tables(meta[om, c])
        tab[om] = table.T.astype(BF)
        high, rest = split(weight)
        wtab[om, c, 0:ROWS, :] = high
        wtab[om, c, ROWS:2 * ROWS, :] = rest

    def make_weights(om, cs):
        _, weight = tables(meta[om, cs])
        high, rest = split(weight)
        wtab[om, cs, 0:ROWS, :] = high
        wtab[om, cs, ROWS:2 * ROWS, :] = rest

    def dispatch(om, k):
        @pl.when(om == 0)
        def _():
            row_load(k).wait()

        @pl.when(om == 1)
        def _():
            zrow(k).wait_recv()

        value = dot(tab[om], rw[om, k]).astype(BF)
        got[om, k, 0, c] = value[0:CAP]
        sel[om, k] = value[CAP:].reshape(3, CAP, KC)
        for d in range(3):
            remote(sel.at[om, k, d], got.at[om, k, d + 1, c], s_x, r_x.at[om, k], x_up[d]).start()

    def forward(om, k):
        return remote(got.at[om, k, :, c], got.at[om, k, :, c],
                      s_fwd.at[om, k], r_fwd.at[om, k], sibling)

    def arrive(om, k):
        wait_bytes(sel.at[om, k], r_x.at[om, k])
        forward(om, k).start()

    def span(st):
        return pl.ds(0, 8 * CAP) if st == 0 else pl.ds((st - 1) * 4 * CAP, 4 * CAP)

    def chosen(st, k):
        if st == 0:
            return got[0, k].reshape(8 * CAP, KC)
        return got[1, k, :, st - 1].reshape(4 * CAP, KC)

    def gate_up(st, k):
        om, rs = min(st, 1), span(st)
        if st == 0:
            forward(0, k).wait_recv()
        else:
            @pl.when(c == 2 - st)
            def _():
                forward(1, k).wait_recv()
        value = chosen(st, k)
        for n in range(4):
            cols = pl.ds(n * 256, 256)
            acc[om, rs, cols] += dot(value, w[k, :, cols])

    def low_rank(st):
        return sum(dot(chosen(st, k), gub[pl.ds(k * KC, KC), :]) for k in range(NK))

    def zrow_start():
        @pl.loop(0, NK)
        def _(k):
            zrow(k).start()

    @pl.when((far == 0) & (c == 0))
    def _():
        zrow_start()

    for copy in loads[2:]:
        copy.wait()
    left64 = onehot(iota((64, 128), 0) == iota((64, 128), 1))
    right64 = onehot(iota((64, 128), 0) + 64 == iota((64, 128), 1))
    pick = onehot(iota((PART, SHARD), 1) == iota((PART, SHARD), 0) + c * PART)
    fac_a[y, zl, c, 0:PART, :] = (
        dot(dot_nt(pick, pack_g[...]).astype(BF), left64)
        + dot(dot_nt(pick, pack_u[...]).astype(BF), right64)).astype(BF)
    rights = jnp.concatenate([ga_v[0].astype(F32), ua_v[0].astype(F32)], axis=0)
    fac_a[y, zl, c, PART:PART + 32, :] = jnp.concatenate(
        [rights[:, 128 * q:128 * q + 128] for q in range(4)], axis=0).astype(BF)

    def fac_y_send(part, zz):
        fac = (fac_a, fac_b)[part]
        for d in range(3):
            remote(fac.at[y, zz, c], fac.at[y, zz, c],
                   s_fac.at[part, 1], r_facy.at[part, d], y_peers[d]).start()

    def fac_z(part):
        fac = (fac_a, fac_b)[part]
        for d in range(3):
            remote(fac.at[y, zl, c], fac.at[y, zl, c],
                   s_fac.at[part, 0], r_facz.at[part, d], z_peers[d]).start()
        fac_y_send(part, zl)

    fac_z(0)

    make_select(0)

    @pl.loop(0, NK)
    def _(k):
        dispatch(0, k)

    turned = dot_nt(pick, pack_d[...]).astype(BF)
    placed = dot(onehot(iota((PART, 32), 0) == iota((PART, 32), 1)), db_v[0]).astype(BF)
    fac_b[y, zl, c] = (dot(turned, left64) + dot(placed, right64)).astype(BF)
    fac_z(1)

    @pl.loop(0, NJ)
    def _(j):
        dw_load(j).start()
        dw_send(j).start()

    acc[...] = jnp.zeros_like(acc)

    def fac_forward(part, yy):
        fac = (fac_a, fac_b)[part]
        return remote(fac.at[yy, :, c], fac.at[yy, :, c],
                      s_fac.at[part, 2], r_facd.at[part, (yy - y + 4) % 4], sibling)

    def fac_y(part):
        fac = (fac_a, fac_b)[part]
        for d in range(3):
            wait_bytes(fac.at[0, 0, 0], r_facz.at[part, d])
            fac_y_send(part, (zl + 3 - d) % 4)
        fac_forward(part, y).start()

    def fac_cross(part):
        fac = (fac_a, fac_b)[part]
        for d in range(3):
            wait_bytes(fac.at[0, :, 0], r_facy.at[part, d])
            fac_forward(part, (y + 3 - d) % 4).start()

    def fac_arrive(part):
        for d in range(4):
            fac_forward(part, (y + d) % 4).wait_recv()

    def hidden(st):
        om, rs = min(st, 1), span(st)
        high, rest = split(low_rank(st))
        both = jnp.concatenate([high, rest], axis=1)
        for n in range(2):
            cols, ups = pl.ds(n * 256, 256), pl.ds(HID + n * 256, 256)
            gate = acc[om, rs, cols] + dot(both, a2[:, cols])
            up = acc[om, rs, ups] + dot(both, a2[:, ups])
            hid[om, c, rs, cols] = (gate / (1.0 + jnp.exp(-gate)) * up).astype(BF)
        hid_send(st).start()

    def hid_send(st):
        part = hid.at[min(st, 1), c, span(st)]
        return remote(part, part, s_hid.at[st], r_hid.at[st], sibling)

    def low_down(st):
        om, rs = min(st, 1), span(st)
        hid_send(st).wait_recv()
        value = dot(hid[om, 0, rs], dbf[0]) + dot(hid[om, 1, rs], dbf[1])
        high, rest = split(value)
        low2 = high.astype(F32) + pltpu.roll(rest.astype(F32), 64, 1)
        return low2.astype(BF)

    def down(st, j, low2):
        om, rs = min(st, 1), span(st)
        da = daf[pl.ds(pl.multiple_of(c * HALF + j * JC, JC), JC), :]
        value = dot(hid[om, 0, rs], dw[0, j]) + dot(hid[om, 1, rs], dw[1, j]) + dot_nt(low2, da)
        value = value.astype(BF)
        if st == 0:
            value = value.reshape(4, 2, CAP, JC)
            back_got[0, j, 0] = value[0]
            back[0, j] = value[1:]
        else:
            value = value.reshape(4, CAP, JC)
            back_got[1, j, 0, st - 1] = value[0]
            back[1, j, :, st - 1] = value[1:]
        for d in range(3):
            if st == 0:
                src, dst = back.at[0, j, d], back_got.at[0, j, d + 1]
            else:
                src, dst = back.at[1, j, d, st - 1], back_got.at[1, j, d + 1, st - 1]
            remote(src, dst, s_ret, r_ret.at[st, j], x_down[d]).start()

    def zret(m, j):
        return remote(zs.at[j, m], zr.at[j, m], s_zret.at[m, j], r_zret.at[m, j], mirror)

    def mix(om, cs, j):
        value = dot(wtab[om, cs], back_got[om, j, :, cs].reshape(4 * CAP, JC))
        return value[0:ROWS] + value[ROWS:]

    def combine(st, j):
        if st == 0:
            wait_bytes(back.at[0, j], r_ret.at[0, j])
            for cs in range(2):
                own[j, cs] = mix(0, cs, j)
        else:
            wait_bytes(back.at[1, j, :, st - 1], r_ret.at[st, j])
            zs[j, st - 1] = mix(1, st - 1, j).astype(BF)
            zret(st - 1, j).start()

    def fin_send(j):
        return remote(fin.at[j], fin_got.at[j], s_fin.at[j], r_fin.at[j], sibling)

    def finish(j):
        zret(0, j).wait_recv()
        zret(1, j).wait_recv()
        fin[j] = (own[j, 1 - c] + zr[j, 1 - c].astype(F32)).astype(BF)
        fin_send(j).start()
        cols = pl.ds(pl.multiple_of(c * HALF + j * JC, JC), JC)
        out[:, cols] = (own[j, c] + zr[j, c].astype(F32)).astype(BF)

    @pl.when((far == 1) & (c == 0))
    def _():
        zrow_start()

    fac_y(0)

    @pl.loop(0, NK + 2)
    def _(k):
        @pl.when(k < NK)
        def _():
            arrive(0, k)

        @pl.when((c == 1) & (k == jnp.where(far == 1, 6, 5)))
        def _():
            zrow_start()

        @pl.when(k == 2)
        def _():
            meta_mirror.wait_recv()
            meta_second.start()
            make_select(1)

        @pl.when(k == 4 - far)
        def _():
            fac_y(1)

        @pl.when((c == 0) & (k >= 3) & (k < NK))
        def _():
            dispatch(1, 2 * k - 6)

            @pl.when(k < NK - 1)
            def _():
                dispatch(1, 2 * k - 5)

        @pl.when(k >= 2)
        def _():
            w_load(k - 2, 0).wait()
            w_load(k - 2, 1).wait()
            gate_up(0, k - 2)

    fac_cross(0)

    meta_sibling.wait_recv()
    make_weights(0, 1 - c)
    meta_second.wait_recv()
    make_weights(1, 1 - c)

    @pl.when((far == 1) & (c == 1))
    def _():
        @pl.loop(0, 4)
        def _(k):
            dispatch(1, k)

    fac_arrive(0)
    for yy in range(4):
        gub[pl.ds(yy * 896, 896), :] = fac_a[yy, :, :, 0:PART, :].reshape(896, 128)
    small = fac_a[:, :, c, PART:PART + 32, :].astype(F32).reshape(16, 4, 8, 128)
    r = iota((128, 128), 0)
    s = iota((128, 128), 1)
    take = onehot((s // 8 == (r % 64) // 4) & (s % 8 == r % 4 + 4 * (r // 64)))
    upper = r < 64
    for q in range(4):
        right = dot(take, small[:, q].reshape(128, 128).astype(BF)).astype(BF)
        none = jnp.zeros_like(right)
        for n in range(2):
            rs = pl.ds(n * 128, 128)
            a2[rs, pl.ds(128 * q, 128)] = jnp.where(upper, right, none)
            a2[rs, pl.ds(HID + 128 * q, 128)] = jnp.where(upper, none, right)
    @pl.when(far == 0)
    def _():
        hidden(0)

        @pl.when(c == 1)
        def _():
            @pl.loop(0, NK)
            def _(k):
                dispatch(1, k)

    @pl.when((far == 1) & (c == 1))
    def _():
        @pl.loop(4, NK)
        def _(k):
            dispatch(1, k)

    @pl.loop(0, NK + 1)
    def _(k):
        @pl.when((c == 0) & (k < NK))
        def _():
            arrive(1, k)

        @pl.when(k == 5)
        def _():
            fac_cross(1)

        @pl.when(k > 0)
        def _():
            gate_up(1, k - 1)

    hidden(1)

    @pl.when(far == 1)
    def _():
        hidden(0)

    fac_arrive(1)
    left = iota((896, 128), 1) < 64
    for yy in range(4):
        part = fac_b[yy].reshape(896, 128).astype(F32)
        part = jnp.where(left, part, 0.0)
        daf[pl.ds(yy * 896, 896), :] = (part + pltpu.roll(part, 64, 1)).astype(BF)
        for core in range(2):
            part = fac_b[yy, :, core, 0:32, :].reshape(128, 128)
            dbf[core, pl.ds(yy * 128, 128), :] = jnp.where(
                iota((128, 128), 1) < 64, jnp.zeros_like(part), part)


    @pl.loop(0, NJ)
    def _(j):
        dw_load(j).wait()
        dw_send(j).wait_recv()

    low_a = low_down(1)

    @pl.loop(0, NJ)
    def _(j):
        down(1, j, low_a)

    @pl.when(c == 1)
    def _():
        @pl.loop(0, NK)
        def _(k):
            arrive(1, k)

    low_own = low_down(0)
    down(0, 0, low_own)
    down(0, 1, low_own)

    @pl.when(far == 1)
    def _():
        combine(1, 0)
        combine(1, 1)

    @pl.when(c == 0)
    def _():
        @pl.loop(0, NK)
        def _(k):
            forward(1, k).wait_recv()

    for n in range(4):
        cols = pl.ds(n * 256, 256)
        acc[1, span(2), cols] = sum(dot(chosen(2, k), w[k, :, cols]) for k in range(NK))
    hidden(2)

    @pl.when(far == 0)
    def _():
        combine(1, 0)
        combine(1, 1)

    combine(1, 2)
    low_b = low_down(2)

    @pl.loop(0, NJ)
    def _(j):
        down(2, j, low_b)

        @pl.when(j < NJ - 3)
        def _():
            combine(1, j + 3)

    @pl.loop(2, NJ)
    def _(j):
        down(0, j, low_own)

    @pl.loop(0, NJ)
    def _(j):
        combine(2, j)

    meta_mirror.wait_send()
    meta_sibling.wait_send()
    meta_second.wait_send()
    wait_bytes(sel, s_x)
    for part, fac in enumerate((fac_a, fac_b)):
        wait_bytes(fac.at[0, pl.ds(0, 3), 0], s_fac.at[part, 0])
        wait_bytes(fac.at[pl.ds(0, 3), :, 0], s_fac.at[part, 1])
        wait_bytes(fac.at[:, :, 0], s_fac.at[part, 2])
    for st in range(3):
        hid_send(st).wait_send()

    @pl.loop(0, NK)
    def _(k):
        forward(0, k).wait_send()
        forward(1, k).wait_send()
        zrow(k).wait_send()
        dw_send(k).wait_send()

    def store_received(j):
        fin_send(j).wait_recv()
        cols = pl.ds(pl.multiple_of((1 - c) * HALF + j * JC, JC), JC)
        out[:, cols] = fin_got[j]

    @pl.loop(0, NJ)
    def _(j):
        combine(0, j)
        finish(j)

        @pl.when(j >= 3)
        def _():
            store_received(j - 3)

    @pl.loop(NJ - 3, NJ)
    def _(j):
        store_received(j)

    wait_bytes(back, s_ret)

    @pl.loop(0, NJ)
    def _(j):
        zret(0, j).wait_send()
        zret(1, j).wait_send()
        fin_send(j).wait_send()


def on_device(rows, ids, wts, gate_w, up_w, down_w, gate_b, gate_a, up_b, up_a, down_b, down_a):
    args = (rows, ids.T, wts.T, gate_w, up_w, down_w, gate_b.swapaxes(1, 2), gate_a,
            up_b.swapaxes(1, 2), up_a, down_b, down_a)
    vmem = pl.BlockSpec(memory_space=pltpu.VMEM)
    hbm = pl.BlockSpec(memory_space=pltpu.HBM)
    dma = pltpu.SemaphoreType.DMA
    scratch = [
        pltpu.VMEM((2, NK, ROWS, KC), BF),
        pltpu.VMEM((2, 2, ROWS, 128), F32),
        pltpu.VMEM((2, 128, ROWS), BF),
        pltpu.VMEM((2, 2, 2 * ROWS, 128), BF),
        pltpu.VMEM((2, NK, 3, CAP, KC), BF),
        pltpu.VMEM((2, NK, 4, 2, CAP, KC), BF),
        pltpu.VMEM((NK, KC, 2 * HID), BF),
        pltpu.VMEM((2, NJ, HID, JC), BF),
        pltpu.VMEM((2, 8 * CAP, 2 * HID), F32),
        pltpu.VMEM((2, 2, 8 * CAP, HID), BF),
        pltpu.VMEM((2, NJ, 3, 2, CAP, JC), BF),
        pltpu.VMEM((2, NJ, 4, 2, CAP, JC), BF),
        pltpu.VMEM((2, ROWS), jnp.int32),
        pltpu.VMEM((2, ROWS), F32),
        pltpu.VMEM((1, 4, HID), BF),
        pltpu.VMEM((1, 4, HID), BF),
        pltpu.VMEM((1, 32, RANK), BF),
        pltpu.VMEM((RANK, SHARD), BF),
        pltpu.VMEM((RANK, SHARD), BF),
        pltpu.VMEM((RANK, SHARD), BF),
        pltpu.VMEM((4, 4, 2, PART + 32, 128), BF),
        pltpu.VMEM((4, 4, 2, PART, 128), BF),
        pltpu.VMEM((D, 128), BF),
        pltpu.VMEM((D, 128), BF),
        pltpu.VMEM((2, HID, 128), BF),
        pltpu.VMEM((256, 2 * HID), BF),
        pltpu.VMEM((NJ, 2, ROWS, JC), BF),
        pltpu.VMEM((NJ, 2, ROWS, JC), BF),
        pltpu.VMEM((NJ, 2, ROWS, JC), F32),
        pltpu.VMEM((NJ, ROWS, JC), BF),
        pltpu.VMEM((NJ, ROWS, JC), BF),
        dma((NK + 8,)),
        dma((NK, 2)),
        dma((NJ,)),
        dma((3,)),
        dma((NK,)),
        dma((NK,)),
        dma((3,)),
        dma,
        dma((2, NK)),
        dma((2, NK)),
        dma((2, NK)),
        dma((NJ,)),
        dma((NJ,)),
        dma((2, 3)),
        dma((2, 3)),
        dma((2, 3)),
        dma((2, 4)),
        dma((3,)),
        dma((3,)),
        dma,
        dma((3, NJ)),
        dma((2, NJ)),
        dma((2, NJ)),
        dma((NJ,)),
        dma((NJ,)),
    ]
    return pl.pallas_call(
        kernel,
        out_shape=jax.ShapeDtypeStruct((ROWS, D), BF),
        in_specs=[hbm] * 12,
        out_specs=vmem,
        scratch_shapes=scratch,
        compiler_params=pltpu.CompilerParams(
            collective_id=0, has_side_effects=True, vmem_limit_bytes=63 << 20),
        cost_estimate=pl.CostEstimate(
            flops=8 << 30, bytes_accessed=13 << 20, transcendentals=1 << 18),
        name="expert_layer",
    )(*args)


def solution(mesh):
    return jax.shard_map(
        on_device,
        mesh=mesh,
        in_specs=(
            P(("group", "expert"), None),
            P(("group", "expert"), None),
            P(("group", "expert"), None),
            P("expert", None, None),
            P("expert", None, None),
            P("expert", None, None),
            P(None, "group", None),
            P("expert", "group", None),
            P(None, "group", None),
            P("expert", "group", None),
            P("expert", "group", None),
            P(None, None, "group"),
        ),
        out_specs=P(("group", "expert"), None),
        check_vma=False,
    )
```
